256 devices in a mesh: lat: 16 (over y, x), tm: 16 (over z, core).
Axes of the slice: x: 4, y: 4, z: 8, core: 2. Of those that a mesh axis runs over, the one named last changes fastest.
Arguments:
- light_field: float32 [2, 1024, 4096], P(None, 'lat', 'tm'), may hold values from -6 to 6
- lateral_phase: float32 [1024], replicated, may hold values from -3.140625 to 3.140625
- spectral_phase: float32 [4096], replicated, may hold values from -3.140625 to 3.140625
- occupation: float32 [128, 1024], P(None, 'lat'), may hold values from -0.5 to 1
- bin_decay: float32 [32], replicated, may hold values from 2e-05 to 0.05
- bin_detune: float32 [32], replicated, may hold values from -0.3 to 0.3
- group_bin: int32 [128], replicated, may hold values from 0 to 31
Outputs:
- output_field: float32 [2, 1024, 4096], P(None, 'lat', 'tm')
The draws below stay inside these ranges and needn't reach their ends.
All inputs are finite; a program needn't handle non-finite values.
Results may differ from the reference program's by a relative error of at most 0.0003.
Values sent between devices are 32-bit elements; how exact they have to be, the bound alone decides.
No kernel may reach another device: no remote copies, remote signals or barrier semaphores. Data moves between devices by JAX's collectives and lax.ppermute only.
A program may use at most 128 MiB of HBM per device.

```python
import math
import jax
import jax.numpy as jnp
from jax import lax

NX = 1024
GROUPS = 128
BINS = 32
STEPS = 2
NT = 4096


def place_ends(drawn, own_key, smallest, top_value):
    dims = drawn.shape
    spot = [jax.random.randint(jax.random.fold_in(own_key, axis), (), 0, dims[axis]) for axis in range(len(dims))]
    drawn = drawn.at[tuple(spot)].set(smallest)
    longest = dims.index(max(dims))
    spot[longest] = (spot[longest] + 1) % dims[longest]
    return drawn.at[tuple(spot)].set(top_value)


def levels(rng, dims, shards, smallest, top_value):
    factor_of = 1.0
    for dim, blocks in shards:
        steps = jax.random.uniform(jax.random.fold_in(jax.random.fold_in(rng, 6), dim), (blocks,), jnp.float32, smallest / len(shards), top_value / len(shards))
        factor_of = factor_of * jnp.repeat(jnp.exp(steps), dims[dim] // blocks).reshape((-1,) + (1,) * (len(dims) - 1 - dim))
    return factor_of


def scatter_about(stream_key, dims, spread, most, pieces=(), kind=jnp.bfloat16):
    entries = jax.random.normal(stream_key, dims, jnp.float32) * spread
    if len(pieces) > 0:
        entries = levels(stream_key, dims, pieces, -0.22, 0.18) * entries
    return jnp.clip(entries, min=-most, max=most).astype(kind)


def setup_inputs(seed: int = 0) -> dict:
    streams_of = jax.random.split(jax.random.key(seed), 8)
    return {
        "light_field": scatter_about(streams_of[0], (2, NX, NT), 1.0, 6.0, ((1, 16), (2, 16)), jnp.float32),
        "lateral_phase": jnp.clip(jax.random.uniform(streams_of[1], (NX,), jnp.float32, -3.140625, 3.140625), -3.140625, 3.140625),
        "spectral_phase": jnp.clip(jax.random.uniform(streams_of[2], (NT,), jnp.float32, -3.140625, 3.140625), -3.140625, 3.140625),
        "occupation": jnp.clip(-0.5 + 1.5 * jax.random.uniform(streams_of[3], (GROUPS, NX), jnp.float32) ** levels(streams_of[3], (GROUPS, NX), ((1, 16),), -0.2, 0.2), -0.5, 1.0),
        "bin_decay": jnp.clip(jnp.exp(jax.random.uniform(streams_of[4], (BINS,), jnp.float32, math.log(1.9999999494757503e-05), math.log(0.05))), 1.9999999494757503e-05, 0.05),
        "bin_detune": jnp.clip(jax.random.uniform(streams_of[5], (BINS,), jnp.float32, -0.3, 0.3), -0.3, 0.3),
        "group_bin": place_ends(jax.random.randint(streams_of[6], (GROUPS,), 0, BINS), jax.random.fold_in(streams_of[6], 1), 0, BINS - 1).astype(jnp.int32),
    }


GAIN_SCALE = 0.5

def reference(light_field, lateral_phase, spectral_phase, occupation, bin_decay, bin_detune, group_bin):
    decay_rate = bin_decay[group_bin]
    detuning = bin_detune[group_bin]
    propagator = jnp.exp(-decay_rate) * (jnp.cos(detuning) - 1j * jnp.sin(detuning))
    drive = jnp.sqrt(-jnp.expm1(-2.0 * decay_rate))
    coupling = drive[:, None] * occupation
    weight = GAIN_SCALE / jnp.sqrt(jnp.float32(occupation.shape[0]))
    current = light_field[0] + 1j * light_field[1]
    lateral_turn = jnp.exp(1j * lateral_phase)[:, None]
    spectral_turn = jnp.exp(1j * spectral_phase)[None, :]

    def advance(polar_state, column):
        polar_state = propagator[:, None] * polar_state + coupling * column[None, :]
        return (polar_state, lax.optimization_barrier(jnp.sum(polar_state, axis=0)))
    for repeat in range(STEPS):
        current = jnp.fft.ifft(jnp.fft.fft(current, axis=0) * lateral_turn, axis=0)
        current = jnp.fft.ifft(jnp.fft.fft(current, axis=1) * spectral_turn, axis=1)
        initial = jnp.zeros(coupling.shape, current.dtype)
        ignored, summed = lax.scan(advance, initial, current.T)
        current = current + 1j * weight * summed.T
    return jnp.stack([jnp.real(current), jnp.imag(current)]).astype(jnp.float32)
```

```python
import math

import jax
import jax.numpy as jnp
import numpy as np
from jax import lax
from jax.experimental import pallas as pl
from jax.experimental.pallas import tpu as pltpu
from jax.sharding import PartitionSpec as P

NX, NT, BINS, GROUPS = 1024, 4096, 32, 128
WEIGHT = 0.5 / math.sqrt(GROUPS)
F32, BF16 = jnp.float32, jnp.bfloat16
BOTH = ("lat", "tm")


def split_table(table):
    high = table.astype(np.float32).astype(jnp.bfloat16)
    low = (table - high.astype(np.float64)).astype(jnp.bfloat16)
    return high, low


def build_tables():
    grid = np.arange
    angle = 2 * np.pi * (grid(256)[:, None] * grid(256)[None, :] % 256) / 256
    wide = np.concatenate([np.cos(angle), np.sin(angle)], 1)
    tall = np.concatenate([np.cos(angle), np.sin(angle)], 0)
    lane = grid(128)
    c, q, col = lane // 64, lane // 16 % 4, lane % 16
    row = grid(128)
    rm, rc, rq = row // 8, row // 4 % 2, row % 4
    turn = 2 * np.pi * (col[:, None] * rm[None, :] % 16) / 16
    same = c[:, None] == rc[None, :]
    sign = np.where(c[:, None] == 0, 1.0, -1.0)
    small = np.where(same, np.cos(turn), sign * np.sin(turn)) * (q[:, None] == rq[None, :])
    short = 2 * np.pi * (col[:64, None] * grid(256)[None, :]) / NT
    index = 16 * grid(256)[:, None] + grid(16)[None, :]
    index = np.where(index > NT // 2, index - NT, index)
    omega = 2 * np.pi * index / NT
    omega_high = omega.astype(np.float32)
    omega_low = (omega - omega_high).astype(np.float32)
    omega_lanes = np.tile(omega, (1, 8))
    eight = lane // 16
    twiddle_a = np.zeros((8, 256, 128))
    twiddle_b = np.zeros((8, 256, 128))
    for r in range(8):
        source = (eight + r) % 8
        sc, sq = source // 4, source % 4
        theta = -2 * np.pi * ((sq - q)[None, :] * grid(256)[:, None]) / NX
        re, im = np.cos(theta), np.sin(theta)
        same_part = (sc == c)[None, :]
        flip = np.where(c == 0, -1.0, 1.0)[None, :]
        twiddle_a[r] = np.where(same_part, re, flip * im) / NX
        twiddle_b[r] = np.where(same_part, -im, flip * re) / NX
    t = {}
    t["wide"] = np.concatenate(split_table(wide), 0)
    t["tall"] = np.concatenate(split_table(tall), 1)
    t["small"] = np.concatenate(split_table(small), 0)
    t["small_back"] = np.concatenate(split_table(small.T), 0)
    t["tc"] = np.cos(short).astype(np.float32)
    t["ts"] = np.sin(short).astype(np.float32)
    t["omega_rows"] = np.stack([omega_high.T, omega_low.T])
    t["omega_lanes"] = np.stack([np.tile(omega_high, (1, 8)), np.tile(omega_low, (1, 8))])
    t["back_re"] = (np.cos(omega_lanes) / NT).astype(np.float32)
    t["back_im"] = (-np.sin(omega_lanes) / NT).astype(np.float32)
    t["twiddle_a"] = twiddle_a.astype(np.float32)
    t["twiddle_b"] = twiddle_b.astype(np.float32)
    return t


TABLES = build_tables()


def iota(shape, dim):
    return lax.broadcasted_iota(jnp.int32, shape, dim)


def halves(value):
    high = value.astype(BF16)
    return high, (value - high.astype(F32)).astype(BF16)


def thirds(value):
    high = value.astype(BF16)
    rest = value - high.astype(F32)
    middle = rest.astype(BF16)
    return high, middle, (rest - middle.astype(F32)).astype(BF16)


def dot(left, right):
    return lax.dot_general(left, right, (((1,), (0,)), ((), ())), preferred_element_type=F32)


def dot_nt(left, right):
    return lax.dot_general(left, right, (((1,), (1,)), ((), ())), preferred_element_type=F32)


def quadrants(product, rows, cols):
    return product[:rows, :cols] + (product[:rows, cols:] + product[rows:, :cols])


def table_times(table, value):
    product = dot(table, jnp.concatenate(halves(value), 1))
    return quadrants(product, table.shape[0] // 2, value.shape[1])


def times_table(value, table):
    product = dot(jnp.concatenate(halves(value), 0), table)
    return quadrants(product, value.shape[0], table.shape[1] // 2)


def sine_cosine_half(angle):
    x = angle * 0.5
    z = x * x
    s = jnp.full_like(z, 1.0 / 6227020800.0)
    for k in (-1.0 / 39916800.0, 1.0 / 362880.0, -1.0 / 5040.0, 1.0 / 120.0, -1.0 / 6.0):
        s = s * z + k
    c = jnp.full_like(z, -1.0 / 87178291200.0)
    for k in (1.0 / 479001600.0, -1.0 / 3628800.0, 1.0 / 40320.0, -1.0 / 720.0, 1.0 / 24.0, -0.5):
        c = c * z + k
    return x + x * (z * s), 1.0 + z * c


def resonance(detune, keep, lost, high, low):
    s, c = sine_cosine_half((detune + high) + low)
    re = lost + (2.0 * keep) * (s * s)
    im = (2.0 * keep) * (s * c)
    scale = 1.0 / (re * re + im * im)
    return re * scale, -(im * scale)


def prepare(params, group_bin, occupation, spectral, lateral, omega_rows, omega_row, phase_row,
            back_re, back_im, twiddle_a, twiddle_b, quad):
    detune, keep, lost, drive = (params[:, k : k + 1] for k in range(4))
    real, imag = [], []
    for w1 in range(16):
        g_re, g_im = resonance(
            detune, keep, lost, omega_rows[0, w1 : w1 + 1, :], omega_rows[1, w1 : w1 + 1, :]
        )
        real.append(g_re)
        imag.append(g_im)
    resonances = jnp.concatenate(halves(jnp.concatenate(real + imag, 0)), 0)
    member = (iota((BINS, GROUPS), 0) == group_bin).astype(BF16)
    per_bin = dot(member, jnp.concatenate(thirds(occupation), 1))
    width = occupation.shape[1]
    per_bin = (per_bin[:, :width] + per_bin[:, width : 2 * width]) + per_bin[:, 2 * width :]
    per_bin = per_bin * drive
    parts = thirds(per_bin)
    pick = (iota((128, 128), 0) == 4 * quad + iota((128, 128), 1) // 16 % 4).astype(BF16)
    chosen = (dot(parts[0], pick) + dot(parts[1], pick)) + dot(parts[2], pick)
    lane = iota((BINS, 128), 1)
    couple_row = jnp.sum(
        jnp.where(iota((BINS, 128), 0) == lane // 64 * 16 + lane % 16, chosen, 0.0),
        axis=0, keepdims=True,
    )
    pick_rows = (iota((64, 128), 1) == 4 * quad + iota((64, 128), 0) // 16).astype(BF16)
    spread = sum(dot_nt(pick_rows, jnp.concatenate([part] * 16, 0)) for part in parts)
    couple_grid = jnp.where(
        iota((64, 512), 1) // 32 == iota((64, 512), 0) % 16, spread, 0.0
    )
    gain_high, gain_low = halves(couple_grid * WEIGHT)
    gain = dot(jnp.concatenate([gain_high, gain_low], 0),
               jnp.concatenate([resonances[:512], resonances[512:1024]], 1))
    gain_rest = dot(gain_high, jnp.concatenate([resonances[1024:1536], resonances[1536:]], 1))
    gain = (gain[:64] + gain[64:]) + gain_rest
    gain = jnp.concatenate([-gain[:, 256:], gain[:, :256]], 0)
    s, c = sine_cosine_half(spectral)
    cos, sin = 1.0 - 2.0 * (s * s), 2.0 * (s * c)
    side = jnp.where(iota((256, 128), 1) < 64, -1.0, 1.0)
    wrap_a = cos * back_re - sin * back_im
    wrap_b = (cos * back_im + sin * back_re) * side
    s, c = sine_cosine_half(lateral)
    cos, sin = 1.0 - 2.0 * (s * s), 2.0 * (s * c)
    r = [cos[:, k : k + 1] for k in range(4)]
    i = [sin[:, k : k + 1] for k in range(4)]
    blocks_re = [
        (r[0] + r[2]) + (r[1] + r[3]),
        (r[0] - r[2]) + (i[1] - i[3]),
        (r[0] + r[2]) - (r[1] + r[3]),
        (r[0] - r[2]) - (i[1] - i[3]),
    ]
    blocks_im = [
        (i[0] + i[2]) + (i[1] + i[3]),
        (i[0] - i[2]) - (r[1] - r[3]),
        (i[0] + i[2]) - (i[1] + i[3]),
        (i[0] - i[2]) + (r[1] - r[3]),
    ]
    mixing = [
        twiddle_a[k] * blocks_re[k % 4] + twiddle_b[k] * blocks_im[k % 4] for k in range(8)
    ]
    rows = jnp.concatenate([params[:16]] * 4 + [params[16:]] * 4, 0)
    g_re, g_im = resonance(
        rows[:, 0:1], rows[:, 1:2], rows[:, 2:3], omega_row[0:1, :], omega_row[1:2, :]
    )
    s, c = sine_cosine_half(phase_row)
    once_re, once_im = 1.0 - 2.0 * (s * s), 2.0 * (s * c)
    twice_re = once_re * once_re - once_im * once_im
    twice_im = 2.0 * once_re * once_im
    inside = iota((128, 128), 0) // 16 % 4 == iota((128, 128), 1) // 16 % 4
    left = iota((128, 128), 1) < 64
    f_re, f_im = -WEIGHT * twice_im, WEIGHT * twice_re
    b_re = jnp.where(inside, g_re * f_re - g_im * f_im, 0.0)
    b_im = jnp.where(inside, g_re * f_im + g_im * f_re, 0.0)
    gain_here = jnp.concatenate([b_re, jnp.where(left, -b_im, b_im)], 1)
    gain_here = jnp.concatenate(halves(gain_here), 1)
    side_row = side[0:1]
    twice = jnp.concatenate([twice_re, twice_im * side_row], 1)
    k_re, k_im = rows[:, 4:5], rows[:, 5:6]
    f_re = once_re * k_re - once_im * k_im
    f_im = once_re * k_im + once_im * k_re
    h_re = jnp.where(inside, g_re * f_re - g_im * f_im, 0.0)
    h_im = jnp.where(inside, g_re * f_im + g_im * f_re, 0.0)
    top, bottom = jnp.where(left, h_re, h_im), jnp.where(left, -h_im, h_re)
    wrap_here = jnp.concatenate([top[:64], bottom[:64], top[64:], bottom[64:]], 0)
    wrap_here = jnp.concatenate(halves(wrap_here), 1)
    return (resonances, couple_row, couple_grid, gain, wrap_a, wrap_b, mixing, gain_here,
            twice, wrap_here)


def half_sign(shape):
    return jnp.where(iota(shape, 1) < 64, -1.0, 1.0)


def wrap_state(resonances, weighted, roll):
    product = dot(resonances, jnp.concatenate(halves(weighted), 1))
    product = quadrants(product, 1024, 128)
    lane = iota((BINS, 128), 1) % 16
    sums = []
    for part in range(2):
        total = jnp.zeros((BINS, 128), F32)
        for w1 in range(16):
            start = (part * 16 + w1) * BINS
            total = total + jnp.where(lane == w1, product[start : start + BINS], 0.0)
        sums.append(total)
    return sums[0] + half_sign((BINS, 128)) * roll(sums[1], 64)


def to_rows(field, couple_row, resonances, wrap_a, wrap_b, wide, small, tc, ts, roll):
    mixed = table_times(small, field)
    re, im = mixed[:64], mixed[64:]
    re, im = re * tc + im * ts, im * tc - re * ts
    both = jnp.concatenate(
        [jnp.concatenate([re, im], 1), jnp.concatenate([im, -re], 1)], 0
    )
    product = dot_nt(wide, jnp.concatenate(halves(both), 0))
    spectrum = quadrants(product, 256, 128)
    weighted = wrap_a * spectrum + wrap_b * roll(spectrum, 64)
    state = wrap_state(resonances, weighted, roll)
    place = (iota((128, 256), 0) // 16 == iota((128, 256), 1) % 128 // 16).astype(BF16)
    parts = dot(jnp.concatenate(thirds(state), 0), place)
    parts = (parts[:BINS] + parts[BINS : 2 * BINS]) + parts[2 * BINS :]
    lane = iota((BINS, 256), 1)
    chosen = iota((BINS, 256), 0) == lane // 128 * 16 + lane % 16
    state_row = jnp.sum(jnp.where(chosen, parts, 0.0), axis=0, keepdims=True)
    tail = jnp.concatenate([state_row, couple_row], 1)
    return jnp.concatenate([spectrum, jnp.broadcast_to(tail, (256, 384))], 1)


def diffract(blocks, wide, mixing, roll):
    sign = half_sign((256, 128))

    def transform(parts, direction):
        columns = []
        for part in parts:
            turned = roll(part, 64) * (sign * (-direction))
            columns += list(halves(jnp.concatenate([part, turned], 0)))
        product = dot(wide, jnp.concatenate(columns, 1))
        return [
            quadrants(product[:, 256 * k : 256 * k + 256], 256, 128) for k in range(len(parts))
        ]

    spectra = transform(blocks, 1.0)
    mixed = []
    for part in spectra:
        total = mixing[0] * part
        for r in range(1, 8):
            total = total + mixing[r] * roll(part, 128 - 16 * r)
        mixed.append(total)
    return transform(mixed, -1.0)


def columns_step(message, wide, mixing, gain_here, twice, wrap_here, roll):
    field, state0, state1, couple = (message[:, 128 * k : 128 * k + 128] for k in range(4))
    field, state0, state1 = diffract([field, state0, state1], wide, mixing, roll)
    factor = times_table(couple, gain_here) + twice
    turned = roll(couple, 64)
    left = iota((256, 128), 1) < 64
    states = jnp.concatenate(
        [state0 * jnp.where(left, couple, turned), state1 * jnp.where(left, turned, couple)], 1
    )
    wrapped = times_table(states, wrap_here)
    field = factor[:, :128] * field + factor[:, 128:] * roll(field, 64) + wrapped
    return diffract([field], wide, mixing, roll)[0]


def to_blocks(spectrum, params, resonances, couple_grid, gain, back_re, back_im, tall,
              small_back, tc, ts, roll):
    sign = half_sign((256, 128))
    weighted = back_re * spectrum + (back_im * sign) * roll(spectrum, 64)
    state = wrap_state(resonances, weighted, roll)
    state = params[:, 4:5] * state + params[:, 5:6] * (
        half_sign((BINS, 128)) * roll(state, 64)
    )
    gather = (iota((128, 128), 0) // 16 == iota((128, 128), 1) // 16).astype(BF16)
    spread = sum(dot_nt(gather, jnp.concatenate([part] * 16, 0)) for part in thirds(state))
    k_re, k_im = couple_grid * spread[:64], couple_grid * spread[64:]
    left = jnp.concatenate(
        [jnp.concatenate([k_re, -k_im], 1), jnp.concatenate([k_im, k_re], 1)], 0
    )
    left_high, left_low = halves(left)
    wrapped = dot(jnp.concatenate([left_high, left_low], 0), resonances[:1024])
    wrapped = (wrapped[:128] + wrapped[128:]) + dot(left_high, resonances[1024:])
    turned = spectrum.T
    re, im = turned[:64], turned[64:]
    gain_re, gain_im = gain[:64], gain[64:]
    out_re = re + (re * gain_re - im * gain_im) + wrapped[:64]
    out_im = im + (re * gain_im + im * gain_re) + wrapped[64:]
    both = jnp.concatenate(
        [jnp.concatenate([out_re, -out_im], 1), jnp.concatenate([out_im, out_re], 1)], 0
    )
    mixed = times_table(both, tall)
    re, im = mixed[:64], mixed[64:]
    mixed = jnp.concatenate([re * tc - im * ts, im * tc + re * ts], 0)
    return table_times(small_back, mixed) * (1.0 / NT)


def lane_roll(value, shift):
    return pltpu.roll(value, shift, 1)


def call(kernel, out_shape, *operands, flops, smem=0):
    in_specs = [pl.BlockSpec(memory_space=pltpu.SMEM)] * smem + [
        pl.BlockSpec(memory_space=pltpu.VMEM)
    ] * (len(operands) - smem)
    several = isinstance(out_shape, tuple)
    out_spec = pl.BlockSpec(memory_space=pltpu.VMEM)
    moved = sum(x.size * x.dtype.itemsize for x in operands)
    return pl.pallas_call(
        kernel,
        out_shape=out_shape,
        in_specs=in_specs,
        out_specs=(out_spec,) * len(out_shape) if several else out_spec,
        compiler_params=pltpu.CompilerParams(vmem_limit_bytes=40 * 1024 * 1024),
        cost_estimate=pl.CostEstimate(flops=flops, bytes_accessed=moved, transcendentals=0),
    )(*operands)


def shape(*dims, dtype=F32):
    return jax.ShapeDtypeStruct(dims, dtype)


def prepare_kernel(place, params, group_bin, occupation, spectral, lateral, omega_rows,
                   omega_lanes, back_re, back_im, twiddle_a, twiddle_b, *outs):
    here, quad = place[0], place[1]
    omega_row = jnp.concatenate(
        [omega_lanes[0, pl.ds(here, 1), :], omega_lanes[1, pl.ds(here, 1), :]], 0
    )
    phase_row = spectral[pl.ds(here, 1), :]
    made = prepare(
        params[...], group_bin[...], occupation[...], spectral[...], lateral[...],
        omega_rows[...], omega_row, phase_row, back_re[...], back_im[...], twiddle_a, twiddle_b,
        quad,
    )
    for out, value in zip(outs, made):
        if isinstance(value, list):
            for k, part in enumerate(value):
                out[k] = part
        else:
            out[...] = value


def rows_kernel(field, couple_row, resonances, wrap_a, wrap_b, wide, small, tc, ts, out):
    out[...] = to_rows(
        field[...], couple_row[...], resonances[...], wrap_a[...], wrap_b[...], wide[...],
        small[...], tc[...], ts[...], lane_roll,
    )


def columns_kernel(message, wide, mixing, gain_here, twice, wrap_here, out):
    out[...] = columns_step(
        message[...], wide[...], mixing, gain_here[...], twice[...], wrap_here[...], lane_roll
    )


def blocks_kernel(spectrum, params, resonances, couple_grid, gain, back_re, back_im, tall,
                  small_back, tc, ts, out):
    out[...] = to_blocks(
        spectrum[...], params[...], resonances[...], couple_grid[...], gain[...], back_re[...],
        back_im[...], tall[...], small_back[...], tc[...], ts[...], lane_roll,
    )


def bin_params(bin_decay, bin_detune):
    keep = jnp.exp(-bin_decay)
    p_re, p_im = keep * jnp.cos(bin_detune), -keep * jnp.sin(bin_detune)
    whole = jnp.exp(-NT * bin_decay)
    r_re = 1.0 - whole * jnp.cos(NT * bin_detune)
    r_im = whole * jnp.sin(NT * bin_detune)
    k_re, k_im = p_re * r_re - p_im * r_im, p_re * r_im + p_im * r_re
    return jnp.stack(
        [
            bin_detune, keep, -jnp.expm1(-bin_decay), jnp.sqrt(-jnp.expm1(-2.0 * bin_decay)),
            WEIGHT * k_im, -WEIGHT * k_re, keep, keep,
        ],
        axis=1,
    )


def parameter_forms(lateral_phase, spectral_phase, occupation, bin_decay, bin_detune, group_bin):
    return (
        bin_params(bin_decay, bin_detune),
        group_bin[None, :],
        jnp.pad(occupation, ((0, 0), (0, 128 - occupation.shape[1]))),
        jnp.tile(spectral_phase.reshape(256, 16), (1, 8)),
        lateral_phase.reshape(4, 256).T,
    )


def on_device(
    light_field, lateral_phase, spectral_phase, occupation, bin_decay, bin_detune, group_bin
):
    t = {name: jnp.asarray(value) for name, value in TABLES.items()}
    lat, tm = lax.axis_index("lat"), lax.axis_index("tm")
    blocks = light_field.reshape(2, 16, 4, 256).transpose(1, 0, 2, 3).reshape(16, 8, 256)
    rows = lax.all_to_all(blocks, "tm", 0, 0, tiled=True).reshape(128, 256)
    forms = parameter_forms(
        lateral_phase, spectral_phase, occupation, bin_decay, bin_detune, group_bin
    )
    place = jnp.stack([lat * 16 + tm, tm]).astype(jnp.int32)
    (resonances, couple_row, couple_grid, gain, wrap_a, wrap_b, mixing, gain_here, twice,
     wrap_here) = call(
        prepare_kernel,
        (
            shape(2048, 256, dtype=BF16), shape(1, 128), shape(64, 512), shape(128, 256),
            shape(256, 128), shape(256, 128), shape(8, 256, 128), shape(128, 512, dtype=BF16),
            shape(1, 256), shape(256, 256, dtype=BF16),
        ),
        place, *forms, t["omega_rows"], t["omega_lanes"], t["back_re"], t["back_im"],
        t["twiddle_a"], t["twiddle_b"],
        flops=200_000_000, smem=1,
    )
    message = call(
        rows_kernel, shape(256, 512),
        rows, couple_row, resonances, wrap_a, wrap_b, t["wide"], t["small"], t["tc"], t["ts"],
        flops=500_000_000,
    )
    message = lax.all_to_all(message, BOTH, 0, 0, tiled=True)
    columns = call(
        columns_kernel, shape(256, 128),
        message, t["wide"], mixing, gain_here, twice, wrap_here,
        flops=1_000_000_000,
    )
    spectrum = lax.all_to_all(columns, BOTH, 0, 0, tiled=True)
    finished = call(
        blocks_kernel, shape(128, 256),
        spectrum, forms[0], resonances, couple_grid, gain, t["back_re"], t["back_im"],
        t["tall"], t["small_back"], t["tc"], t["ts"],
        flops=800_000_000,
    )
    turned = lax.all_to_all(finished.reshape(16, 8, 256), "tm", 0, 0, tiled=True)
    return turned.reshape(16, 2, 4, 256).transpose(1, 0, 2, 3).reshape(2, 64, 256)


def solution(mesh):
    return jax.shard_map(
        on_device,
        mesh=mesh,
        in_specs=(P(None, "lat", "tm"), P(), P(), P(None, "lat"), P(), P(), P()),
        out_specs=P(None, "lat", "tm"),
        check_vma=False,
    )
```

```python
import math

import jax
import jax.numpy as jnp
import numpy as np
from jax import lax
from jax.experimental import pallas as pl
from jax.experimental.pallas import tpu as pltpu
from jax.sharding import PartitionSpec as P

NX, NT, BINS, GROUPS = 1024, 4096, 32, 128
WEIGHT = 0.5 / math.sqrt(GROUPS)
F32, BF16 = jnp.float32, jnp.bfloat16
BOTH = ("lat", "tm")


def split_table(table):
    high = table.astype(np.float32).astype(jnp.bfloat16)
    low = (table - high.astype(np.float64)).astype(jnp.bfloat16)
    return high, low


def build_tables():
    grid = np.arange
    angle = 2 * np.pi * (grid(256)[:, None] * grid(256)[None, :] % 256) / 256
    wide = np.concatenate([np.cos(angle), np.sin(angle)], 1)
    tall = np.concatenate([np.cos(angle), np.sin(angle)], 0)
    lane = grid(128)
    c, q, col = lane // 64, lane // 16 % 4, lane % 16
    to, row = grid(256), grid(256)
    th, tc, tq, tw = to // 128, to // 64 % 2, to // 16 % 4, to % 16
    rm, rc, rh, rq = row // 16, row // 8 % 2, row // 4 % 2, row % 4
    turn = 2 * np.pi * (tw[:, None] * rm[None, :] % 16) / 16
    sign = np.where(tc[:, None] == 0, 1.0, -1.0)
    small = np.where(tc[:, None] == rc[None, :], np.cos(turn), sign * np.sin(turn))
    small = small * (tq[:, None] == rq[None, :]) * (th[:, None] == rh[None, :])
    short = 2 * np.pi * (col[:64, None] * grid(256)[None, :]) / NT
    omega_lanes = np.tile(2 * np.pi * (16 * grid(256)[:, None] + grid(16)[None, :]) / NT, (1, 8))
    eight = lane // 16
    twiddle_a = np.zeros((8, 256, 128))
    twiddle_b = np.zeros((8, 256, 128))
    for r in range(8):
        source = (eight + r) % 8
        sc, sq = source // 4, source % 4
        theta = -2 * np.pi * ((sq - q)[None, :] * grid(256)[:, None]) / NX
        re, im = np.cos(theta), np.sin(theta)
        same_part = (sc == c)[None, :]
        flip = np.where(c == 0, -1.0, 1.0)[None, :]
        twiddle_a[r] = np.where(same_part, re, flip * im) / NX
        twiddle_b[r] = np.where(same_part, -im, flip * re) / NX
    t = {}
    t["wide"] = np.concatenate(split_table(wide), 0)
    t["small"] = np.concatenate(split_table(small), 0)
    t["back"] = np.concatenate(split_table(tall) + split_table(small.T), 0)
    t["twist"] = np.concatenate([np.cos(short), np.sin(short)], 0).astype(np.float32)
    omega_part = np.concatenate([np.cos(omega_lanes), -np.sin(omega_lanes)], 0)
    t["shift"] = (omega_part / NT).astype(np.float32)
    t["twiddle_a"] = twiddle_a.astype(np.float32)
    t["twiddle_b"] = twiddle_b.astype(np.float32)
    return t


STEP = 2 * math.pi / NT
STEP_HIGH = round(STEP * 2**22) / 2**22
STEP_LOW = STEP - STEP_HIGH
TURN = (6.28125, 2 * math.pi - 6.28125)
TABLES = build_tables()


def iota(shape, dim):
    return lax.broadcasted_iota(jnp.int32, shape, dim)


def halves(value):
    high = value.astype(BF16)
    return high, (value - high.astype(F32)).astype(BF16)


def thirds(value):
    high = value.astype(BF16)
    rest = value - high.astype(F32)
    middle = rest.astype(BF16)
    return high, middle, (rest - middle.astype(F32)).astype(BF16)


def dot(left, right):
    return lax.dot_general(left, right, (((1,), (0,)), ((), ())), preferred_element_type=F32)


def dot_nt(left, right):
    return lax.dot_general(left, right, (((1,), (1,)), ((), ())), preferred_element_type=F32)


def quadrants(product, rows, cols):
    return product[:rows, :cols] + (product[:rows, cols:] + product[rows:, :cols])


def table_times(table, value):
    product = dot(table, jnp.concatenate(halves(value), 1))
    return quadrants(product, table.shape[0] // 2, value.shape[1])


def times_table(value, table):
    product = dot(jnp.concatenate(halves(value), 0), table)
    return quadrants(product, value.shape[0], table.shape[1] // 2)


def sine_cosine_half(angle):
    x = angle * 0.5
    z = x * x
    s = jnp.full_like(z, 1.0 / 6227020800.0)
    for k in (-1.0 / 39916800.0, 1.0 / 362880.0, -1.0 / 5040.0, 1.0 / 120.0, -1.0 / 6.0):
        s = s * z + k
    c = jnp.full_like(z, -1.0 / 87178291200.0)
    for k in (1.0 / 479001600.0, -1.0 / 3628800.0, 1.0 / 40320.0, -1.0 / 720.0, 1.0 / 24.0, -0.5):
        c = c * z + k
    return x + x * (z * s), 1.0 + z * c


def resonance(detune, keep, lost, index):
    index = jnp.where(index > NT // 2, index - NT, index).astype(F32)
    s, c = sine_cosine_half((detune + index * STEP_HIGH) + index * STEP_LOW)
    re = lost + (2.0 * keep) * (s * s)
    im = (2.0 * keep) * (s * c)
    scale = 1.0 / (re * re + im * im)
    return re * scale, -(im * scale)


def cosine_sine(angle):
    s, c = sine_cosine_half(angle)
    return 1.0 - 2.0 * (s * s), 2.0 * (s * c)


def lost_by(rate):
    total = jnp.full_like(rate, 1.0 / 5040.0)
    for k in (-1.0 / 720.0, 1.0 / 120.0, -1.0 / 24.0, 1.0 / 6.0, -0.5, 1.0):
        total = k + rate * total
    return rate * total


def exact_dot(left, right):
    parts = thirds(left)
    return (dot(parts[0], right) + dot(parts[1], right)) + dot(parts[2], right)


def pick_dot(left, right):
    parts = thirds(right)
    return (dot(left, parts[0]) + dot(left, parts[1])) + dot(left, parts[2])


def pick_dot_nt(left, right):
    parts = thirds(right)
    return (dot_nt(left, parts[0]) + dot_nt(left, parts[1])) + dot_nt(left, parts[2])


def bin_columns(decay, detune):
    lost = lost_by(decay)
    keep = 1.0 - lost
    drive = jnp.sqrt(lost_by(2.0 * decay))
    cos, sin = cosine_sine(detune)
    p_re, p_im = keep * cos, -keep * sin
    whole = jnp.exp(-float(NT) * decay)
    far = float(NT) * detune
    turns = jnp.floor(far * (0.5 / math.pi) + 0.5)
    cos, sin = cosine_sine((far - turns * TURN[0]) - turns * TURN[1])
    r_re, r_im = 1.0 - whole * cos, whole * sin
    k_re, k_im = p_re * r_re - p_im * r_im, p_re * r_im + p_im * r_re
    rows = jnp.concatenate(
        [detune, keep, lost, drive, WEIGHT * k_im, -WEIGHT * k_re, keep, keep], 0
    )
    eye = (iota((BINS, BINS), 0) == iota((BINS, BINS), 1)).astype(BF16)
    return pick_dot_nt(eye, rows)


def prepare(decay, detune_row, group_bin, occupation, spectral, lateral, shift, twiddle_a,
            twiddle_b, here, quad):
    params = bin_columns(decay, detune_row)
    detune, keep, lost, drive = (params[:, k : k + 1] for k in range(4))
    real, imag = [], []
    for w1 in range(16):
        g_re, g_im = resonance(detune, keep, lost, 16 * iota((BINS, 256), 1) + w1)
        real.append(g_re)
        imag.append(g_im)
    resonances = jnp.concatenate(halves(jnp.concatenate(real + imag, 0)), 0)
    member = (iota((BINS, GROUPS), 0) == group_bin).astype(BF16)
    per_bin = pick_dot(member, occupation) * drive
    points = occupation.shape[1]
    pick = iota((points, 128), 0) == 4 * quad + iota((points, 128), 1) // 16 % 4
    chosen = exact_dot(per_bin, pick.astype(BF16))
    lane = iota((BINS, 128), 1)
    couple_row = jnp.sum(
        jnp.where(iota((BINS, 128), 0) == lane // 64 * 16 + lane % 16, chosen, 0.0),
        axis=0, keepdims=True,
    )
    pick_rows = iota((64, points), 1) == 4 * quad + iota((64, points), 0) // 16
    spread = pick_dot_nt(pick_rows.astype(BF16), jnp.concatenate([per_bin] * 16, 0))
    couple_grid = jnp.where(
        iota((64, 512), 1) // 32 == iota((64, 512), 0) % 16, spread, 0.0
    )
    gain_high, gain_low = halves(couple_grid * WEIGHT)
    gain = dot(jnp.concatenate([gain_high, gain_low], 0),
               jnp.concatenate([resonances[:512], resonances[512:1024]], 1))
    gain_rest = dot(gain_high, jnp.concatenate([resonances[1024:1536], resonances[1536:]], 1))
    gain = (gain[:64] + gain[64:]) + gain_rest
    gain = jnp.concatenate([-gain[:, 256:], gain[:, :256]], 0)
    cos, sin = cosine_sine(spectral)
    row_of = (iota((256, 32), 0) // 8 == iota((256, 32), 1)).astype(BF16)
    mine = iota((256, 128), 1) // 16 == iota((256, 128), 0) % 8
    lane_of = (iota((128, 128), 0) % 16 == iota((128, 128), 1) % 16).astype(BF16)
    cos = exact_dot(jnp.where(mine, pick_dot(row_of, cos), 0.0), lane_of)
    sin = exact_dot(jnp.where(mine, pick_dot(row_of, sin), 0.0), lane_of)
    side = jnp.where(iota((256, 128), 1) < 64, -1.0, 1.0)
    wrap_a = cos * shift[:256] - sin * shift[256:]
    wrap_b = (cos * shift[256:] + sin * shift[:256]) * side
    own = iota((256, 128), 0) == here
    once_re = jnp.sum(jnp.where(own, cos, 0.0), axis=0, keepdims=True)
    once_im = jnp.sum(jnp.where(own, sin, 0.0), axis=0, keepdims=True)
    eye = (iota((128, 128), 0) == iota((128, 128), 1)).astype(BF16)
    cos, sin = cosine_sine(lateral)
    cos, sin = pick_dot_nt(eye, cos), pick_dot_nt(eye, sin)
    r, i = (
        [
            jnp.concatenate([x[:, 2 * k : 2 * k + 1], x[:, 2 * k + 1 : 2 * k + 2]], 0)
            for k in range(4)
        ]
        for x in (cos, sin)
    )
    blocks_re = [
        (r[0] + r[2]) + (r[1] + r[3]),
        (r[0] - r[2]) + (i[1] - i[3]),
        (r[0] + r[2]) - (r[1] + r[3]),
        (r[0] - r[2]) - (i[1] - i[3]),
    ]
    blocks_im = [
        (i[0] + i[2]) + (i[1] + i[3]),
        (i[0] - i[2]) - (r[1] - r[3]),
        (i[0] + i[2]) - (i[1] + i[3]),
        (i[0] - i[2]) + (r[1] - r[3]),
    ]
    mixing = jnp.concatenate(
        [twiddle_a[k] * blocks_re[k % 4] + twiddle_b[k] * blocks_im[k % 4] for k in range(8)], 0
    )
    rows = jnp.concatenate([params[:16]] * 4 + [params[16:]] * 4, 0)
    g_re, g_im = resonance(
        rows[:, 0:1], rows[:, 1:2], rows[:, 2:3], 16 * here + iota((128, 128), 1) % 16
    )
    twice_re = once_re * once_re - once_im * once_im
    twice_im = 2.0 * once_re * once_im
    inside = iota((128, 128), 0) // 16 % 4 == iota((128, 128), 1) // 16 % 4
    left = iota((128, 128), 1) < 64
    f_re, f_im = -WEIGHT * twice_im, WEIGHT * twice_re
    b_re = jnp.where(inside, g_re * f_re - g_im * f_im, 0.0)
    b_im = jnp.where(inside, g_re * f_im + g_im * f_re, 0.0)
    gain_here = jnp.concatenate([b_re, jnp.where(left, -b_im, b_im)], 1)
    gain_here = jnp.concatenate(halves(gain_here), 0)
    side_row = side[0:1]
    twice = jnp.concatenate([twice_re] * 8 + [twice_im * side_row] * 8, 0)
    k_re, k_im = rows[:, 4:5], rows[:, 5:6]
    f_re = once_re * k_re - once_im * k_im
    f_im = once_re * k_im + once_im * k_re
    h_re = jnp.where(inside, g_re * f_re - g_im * f_im, 0.0)
    h_im = jnp.where(inside, g_re * f_im + g_im * f_re, 0.0)
    top, bottom = jnp.where(left, h_re, h_im), jnp.where(left, -h_im, h_re)
    wrap_here = jnp.concatenate([top[:64], bottom[:64], top[64:], bottom[64:]], 0)
    wrap_here = jnp.concatenate(halves(wrap_here), 1)
    first = jnp.concatenate([wrap_a, wrap_b, jnp.broadcast_to(couple_row, (8, 128))], 0)
    second = jnp.concatenate([twice, mixing], 0)
    second_tables = jnp.concatenate([gain_here, wrap_here], 0)
    turned = [jnp.broadcast_to(params[:, k : k + 1], (BINS, 128)) for k in (4, 5)]
    third = jnp.concatenate(
        [couple_grid[:, 128 * k : 128 * k + 128] for k in range(4)]
        + [gain[:, :128], gain[:, 128:]] + turned, 0,
    )
    return resonances, first, second, second_tables, third


def half_sign(shape):
    return jnp.where(iota(shape, 1) < 64, -1.0, 1.0)


def wrap_state(resonances, weighted, roll):
    product = dot(resonances, jnp.concatenate(halves(weighted), 1))
    product = quadrants(product, 1024, 128)
    lane = iota((BINS, 128), 1) % 16
    sums = []
    for part in range(2):
        total = jnp.zeros((BINS, 128), F32)
        for w1 in range(16):
            start = (part * 16 + w1) * BINS
            total = total + jnp.where(lane == w1, product[start : start + BINS], 0.0)
        sums.append(total)
    return sums[0] + half_sign((BINS, 128)) * roll(sums[1], 64)


def to_rows(field, first, resonances, wide, small, twist, roll):
    mixed = table_times(small[...], field)
    mixed = jnp.concatenate([mixed[:128], mixed[128:]], 1)
    re, im = mixed[:64], mixed[64:]
    tc, ts = twist[:64], twist[64:]
    re, im = re * tc + im * ts, im * tc - re * ts
    both = jnp.concatenate(
        [jnp.concatenate([re, im], 1), jnp.concatenate([im, -re], 1)], 0
    )
    product = dot_nt(wide[...], jnp.concatenate(halves(both), 0))
    spectrum = quadrants(product, 256, 128)
    weighted = first[:256] * spectrum + first[256:512] * roll(spectrum, 64)
    state = wrap_state(resonances[...], weighted, roll)
    place = (iota((128, 256), 0) // 16 == iota((128, 256), 1) % 128 // 16).astype(BF16)
    parts = exact_dot(state, place)
    lane = iota((BINS, 256), 1)
    chosen = iota((BINS, 256), 0) == lane // 128 * 16 + lane % 16
    state_row = jnp.sum(jnp.where(chosen, parts, 0.0), axis=0, keepdims=True)
    return spectrum, state_row[:, :128], state_row[:, 128:], first[512:513]


def diffract(blocks, wide, mixing, roll):
    sign = half_sign((256, 128))

    def transform(parts, direction):
        columns = []
        for part in parts:
            turned = roll(part, 64) * (sign * (-direction))
            columns += list(halves(jnp.concatenate([part, turned], 0)))
        product = dot(wide, jnp.concatenate(columns, 1))
        return [
            quadrants(product[:, 256 * k : 256 * k + 256], 256, 128) for k in range(len(parts))
        ]

    spectra = transform(blocks, 1.0)
    mixed = []
    for part in spectra:
        total = mixing[0] * part
        for r in range(1, 8):
            total = total + mixing[r] * roll(part, 128 - 16 * r)
        mixed.append(total)
    return transform(mixed, -1.0)


def columns_step(message, wide, second, second_tables, roll):
    field, state0, state1, couple = message
    mixing = [second[16 + 256 * k : 272 + 256 * k] for k in range(8)]
    field, state0, state1 = diffract([field, state0, state1], wide, mixing, roll)
    product = dot(jnp.concatenate(halves(couple), 0), second_tables[:128])
    rest = dot(couple.astype(BF16), second_tables[128:256])
    factor = (product[:256] + product[256:]) + rest
    turned = roll(couple, 64)
    left = iota((256, 128), 1) < 64
    states = jnp.concatenate(
        [state0 * jnp.where(left, couple, turned), state1 * jnp.where(left, turned, couple)], 1
    )
    wrapped = times_table(states, second_tables[256:])
    straight, crossed = factor[:, :128] + second[0:1], factor[:, 128:] + second[8:9]
    field = straight * field + crossed * roll(field, 64) + wrapped
    return diffract([field], wide, mixing, roll)[0]


def to_blocks(spectrum, resonances, third, back, twist, shift, roll):
    sign = half_sign((256, 128))
    weighted = shift[:256] * spectrum + (shift[256:] * sign) * roll(spectrum, 64)
    state = wrap_state(resonances[...], weighted, roll)
    state = third[512:544] * state + third[544:576] * (
        half_sign((BINS, 128)) * roll(state, 64)
    )
    gather = (iota((128, 128), 0) // 16 == iota((128, 128), 1) // 16).astype(BF16)
    spread = sum(dot_nt(gather, jnp.concatenate([part] * 16, 0)) for part in thirds(state))
    couple_grid = jnp.concatenate([third[64 * k : 64 * k + 64] for k in range(4)], 1)
    k_re, k_im = couple_grid * spread[:64], couple_grid * spread[64:]
    left = jnp.concatenate(
        [jnp.concatenate([k_re, -k_im], 1), jnp.concatenate([k_im, k_re], 1)], 0
    )
    left_high, left_low = halves(left)
    wrapped = dot(jnp.concatenate([left_high, left_low], 0), resonances[:1024])
    wrapped = (wrapped[:128] + wrapped[128:]) + dot(left_high, resonances[1024:])
    turned = spectrum.T
    re, im = turned[:64], turned[64:]
    gain = jnp.concatenate([third[256:384], third[384:512]], 1)
    gain_re, gain_im = gain[:64], gain[64:]
    out_re = re + (re * gain_re - im * gain_im) + wrapped[:64]
    out_im = im + (re * gain_im + im * gain_re) + wrapped[64:]
    both = jnp.concatenate(
        [jnp.concatenate([out_re, -out_im], 1), jnp.concatenate([out_im, out_re], 1)], 0
    )
    high, low = halves(both)
    mixed = dot(jnp.concatenate([high, low], 0), back[:512])
    mixed = (mixed[:128] + mixed[128:]) + dot(high, back[512:1024])
    re, im = mixed[:64], mixed[64:]
    tc, ts = twist[:64], twist[64:]
    re, im = re * tc - im * ts, im * tc + re * ts
    mixed = jnp.concatenate(
        [re[:, :128], im[:, :128], re[:, 128:], im[:, 128:]], 0
    ) * (1.0 / NT)
    return table_times(back[1024:], mixed)


def lane_roll(value, shift):
    return pltpu.roll(value, shift, 1)


def shape(*dims, dtype=F32):
    return jax.ShapeDtypeStruct(dims, dtype)


VMEM_SPEC = pl.BlockSpec(memory_space=pltpu.VMEM)
HBM_SPEC = pl.BlockSpec(memory_space=pltpu.HBM)


def call(kernel, out_shape, in_specs, out_specs, scratch, *operands, flops):
    moved = sum(x.size * x.dtype.itemsize for x in operands)
    return pl.pallas_call(
        kernel,
        out_shape=out_shape,
        in_specs=in_specs,
        out_specs=out_specs,
        scratch_shapes=scratch,
        compiler_params=pltpu.CompilerParams(vmem_limit_bytes=40 * 1024 * 1024),
        cost_estimate=pl.CostEstimate(flops=flops, bytes_accessed=moved, transcendentals=0),
    )(*operands)


def fetches(sources, targets, sems):
    copies = [
        pltpu.make_async_copy(source, target, sems.at[k])
        for k, (source, target) in enumerate(zip(sources, targets))
    ]
    for copy in copies:
        copy.start()
    return copies


def halves_of_tiles(upper, lower):
    low = iota((8, 128), 0) < 4
    return (
        jnp.where(low, upper, pltpu.roll(lower, 4, 0)),
        jnp.where(low, pltpu.roll(upper, 4, 0), lower),
    )


def cut_kernel(field, out, buffer, sems):
    copies = [
        pltpu.make_async_copy(field.at[c], buffer.at[c], sems.at[c]) for c in range(2)
    ]
    for copy in copies:
        copy.start()
    for c in range(2):
        copies[c].wait()
        for row in range(8):
            tile = buffer[c, 8 * row : 8 * row + 8, :]
            first, second = halves_of_tiles(tile[:, :128], tile[:, 128:])
            out[32 * row + 8 * c : 32 * row + 8 * c + 8, :] = first
            out[32 * row + 16 + 8 * c : 32 * row + 24 + 8 * c, :] = second


def join_kernel(rows, field, buffer, sems):
    copies = []
    for c in range(2):
        for row in range(8):
            first = rows[32 * row + 8 * c : 32 * row + 8 * c + 8, :]
            second = rows[32 * row + 16 + 8 * c : 32 * row + 24 + 8 * c, :]
            upper, lower = halves_of_tiles(first, second)
            buffer[c, 8 * row : 8 * row + 8, :128] = upper
            buffer[c, 8 * row : 8 * row + 8, 128:] = lower
        copies.append(pltpu.make_async_copy(buffer.at[c], field.at[c], sems.at[c]))
        copies[-1].start()
    for copy in copies:
        copy.wait()


PREPARED = (
    shape(2048, 256, dtype=BF16), shape(520, 128), shape(2064, 128), shape(512, 256, dtype=BF16),
    shape(576, 128),
)


def prepare_kernel(*refs):
    inputs, outs = refs[:9], refs[9:14]
    local, made, in_sems, out_sems = refs[14:23], refs[23:28], refs[28], refs[29]
    copies = fetches(inputs, local, in_sems)
    for copy in copies:
        copy.wait()
    decay, detune, group, occupation, spectral, lateral, shift, twiddle_a, twiddle_b = local
    quad = lax.axis_index("tm")
    here = lax.axis_index("lat") * 16 + quad
    values = prepare(
        decay[...], detune[...], group[...], occupation[...], spectral[...], lateral[...],
        shift[...], twiddle_a, twiddle_b, here, quad,
    )
    for ref, value in zip(made, values):
        ref[...] = value
    for copy in fetches(made, outs, out_sems):
        copy.wait()


class Late:
    def __init__(self, copy, ref):
        self.copy, self.ref = copy, ref

    def __getitem__(self, index):
        if self.copy is not None:
            self.copy.wait()
            self.copy = None
        return self.ref[index]


def rows_kernel(field, first, resonances, wide, small, twist, out, *scratch):
    local, sems = scratch[:5], scratch[5]
    sources = (small, twist, wide, first, resonances)
    copies = fetches(sources, local, sems)
    small, twist, wide, first, resonances = (Late(*pair) for pair in zip(copies, local))
    spectrum, *rest = to_rows(field[...], first, resonances, wide, small, twist, lane_roll)
    out[pl.ds(0, 256, stride=4), :] = spectrum
    for k, row in enumerate(rest):
        out[pl.ds(k + 1, 256, stride=4), :] = jnp.broadcast_to(row, (256, 128))


def columns_kernel(message, wide, second, second_tables, out):
    parts = [message[pl.ds(k, 256, stride=4), :] for k in range(4)]
    out[...] = columns_step(parts, wide[...], second, second_tables[...], lane_roll)


def blocks_kernel(spectrum, resonances, third, back, twist, shift, out):
    out[...] = to_blocks(
        spectrum[...], resonances[...], third[...], back[...], twist[...], shift[...], lane_roll
    )


def buffers(operands):
    return [pltpu.VMEM(x.shape, x.dtype) for x in operands]


def on_device(
    light_field, lateral_phase, spectral_phase, occupation, bin_decay, bin_detune, group_bin
):
    t = {name: jnp.asarray(value) for name, value in TABLES.items()}
    sems = pltpu.SemaphoreType.DMA
    rows = call(
        cut_kernel, shape(256, 128), [HBM_SPEC], VMEM_SPEC,
        [pltpu.VMEM((2, 64, 256), F32), sems((2,))], light_field, flops=1000,
    )
    rows = lax.all_to_all(rows.reshape(16, 16, 128), "tm", 0, 0, tiled=True)
    arguments = (
        bin_decay[None, :], bin_detune[None, :], group_bin[None, :], occupation,
        spectral_phase.reshape(32, 128), lateral_phase.reshape(8, 128), t["shift"],
        t["twiddle_a"], t["twiddle_b"],
    )
    resonances, first, second, second_tables, third = call(
        prepare_kernel, PREPARED, [HBM_SPEC] * 9, (HBM_SPEC,) * 5,
        buffers(arguments) + buffers(PREPARED) + [sems((9,)), sems((5,))],
        *arguments, flops=200_000_000,
    )
    operands = (first, resonances, t["wide"], t["small"], t["twist"])
    message = call(
        rows_kernel, shape(1024, 128), [VMEM_SPEC] + [HBM_SPEC] * 5, VMEM_SPEC,
        buffers((t["small"], t["twist"], t["wide"], first, resonances)) + [sems((5,))],
        rows.reshape(256, 128), *operands, flops=500_000_000,
    )
    message = lax.all_to_all(message.reshape(256, 4, 128), BOTH, 0, 0, tiled=True)
    columns = call(
        columns_kernel, shape(256, 128), [VMEM_SPEC] * 4, VMEM_SPEC, [],
        message.reshape(1024, 128), t["wide"], second, second_tables, flops=1_000_000_000,
    )
    spectrum = lax.all_to_all(columns, BOTH, 0, 0, tiled=True)
    finished = call(
        blocks_kernel, shape(256, 128), [VMEM_SPEC] * 6, VMEM_SPEC, [],
        spectrum, resonances, third, t["back"], t["twist"], t["shift"], flops=800_000_000,
    )
    turned = lax.all_to_all(finished.reshape(16, 16, 128), "tm", 0, 0, tiled=True)
    return call(
        join_kernel, shape(2, 64, 256), [VMEM_SPEC], HBM_SPEC,
        [pltpu.VMEM((2, 64, 256), F32), sems((2,))], turned.reshape(256, 128), flops=1000,
    )


def solution(mesh):
    return jax.shard_map(
        on_device,
        mesh=mesh,
        in_specs=(P(None, "lat", "tm"), P(), P(), P(None, "lat"), P(), P(), P()),
        out_specs=P(None, "lat", "tm"),
        check_vma=False,
    )
```

```python
import math

import jax
import jax.numpy as jnp
import numpy as np
from jax import lax
from jax.experimental import pallas as pl
from jax.experimental.pallas import tpu as pltpu
from jax.sharding import PartitionSpec as P

NX, NT, BINS, GROUPS = 1024, 4096, 32, 128
WEIGHT = 0.5 / math.sqrt(GROUPS)
F32, BF16 = jnp.float32, jnp.bfloat16
BOTH = ("lat", "tm")


def split_table(table):
    high = table.astype(np.float32).astype(jnp.bfloat16)
    low = (table - high.astype(np.float64)).astype(jnp.bfloat16)
    return high, low


def build_tables():
    grid = np.arange
    angle = 2 * np.pi * (grid(256)[:, None] * grid(256)[None, :] % 256) / 256
    wide = np.concatenate([np.cos(angle), np.sin(angle)], 1)
    tall = np.concatenate([np.cos(angle), np.sin(angle)], 0)
    lane = grid(128)
    c, q, col = lane // 64, lane // 16 % 4, lane % 16
    to, row = grid(256), grid(256)
    th, tc, tq, tw = to // 128, to // 64 % 2, to // 16 % 4, to % 16
    rm, rc, rh, rq = row // 16, row // 8 % 2, row // 4 % 2, row % 4
    turn = 2 * np.pi * (tw[:, None] * rm[None, :] % 16) / 16
    sign = np.where(tc[:, None] == 0, 1.0, -1.0)
    small = np.where(tc[:, None] == rc[None, :], np.cos(turn), sign * np.sin(turn))
    small = small * (tq[:, None] == rq[None, :]) * (th[:, None] == rh[None, :])
    short = 2 * np.pi * (col[:64, None] * grid(256)[None, :]) / NT
    omega_lanes = np.tile(2 * np.pi * (16 * grid(256)[:, None] + grid(16)[None, :]) / NT, (1, 8))
    twiddle = []
    for k in range(1, 4):
        theta = -2 * np.pi * (((q + k) % 4 - q)[None, :] * grid(256)[:, None]) / NX
        twiddle += [np.cos(theta), np.sin(theta)]
    t = {}
    t["ahead"] = np.concatenate(
        [np.concatenate(split_table(x), 0) for x in (wide, small)], 1
    )
    t["back"] = np.concatenate(split_table(tall) + split_table(small.T), 0)
    twist = np.concatenate([np.cos(short), np.sin(short)], 0)
    omega_part = np.concatenate([np.cos(omega_lanes), -np.sin(omega_lanes)], 0)
    twist = [twist[:, :128], twist[:, 128:]]
    t["shift"] = np.concatenate([omega_part / NT] + twist, 0).astype(np.float32)
    t["twiddle"] = np.concatenate(twiddle + twist, 0).astype(np.float32)
    return t


STEP = 2 * math.pi / NT
STEP_HIGH = round(STEP * 2**22) / 2**22
STEP_LOW = STEP - STEP_HIGH
TURN = (6.28125, 2 * math.pi - 6.28125)
TABLES = build_tables()


def iota(shape, dim):
    return lax.broadcasted_iota(jnp.int32, shape, dim)


def halves(value):
    high = value.astype(BF16)
    return high, (value - high.astype(F32)).astype(BF16)


def thirds(value):
    high = value.astype(BF16)
    rest = value - high.astype(F32)
    middle = rest.astype(BF16)
    return high, middle, (rest - middle.astype(F32)).astype(BF16)


def dot(left, right):
    return lax.dot_general(left, right, (((1,), (0,)), ((), ())), preferred_element_type=F32)


def dot_nt(left, right):
    return lax.dot_general(left, right, (((1,), (1,)), ((), ())), preferred_element_type=F32)


def quadrants(product, rows, cols):
    return product[:rows, :cols] + (product[:rows, cols:] + product[rows:, :cols])


def table_times(table, value):
    product = dot(table, jnp.concatenate(halves(value), 1))
    return quadrants(product, table.shape[0] // 2, value.shape[1])


def times_table(value, table):
    product = dot(jnp.concatenate(halves(value), 0), table)
    return quadrants(product, value.shape[0], table.shape[1] // 2)


def sine_cosine_half(angle):
    x = angle * 0.5
    z = x * x
    s = jnp.full_like(z, 1.0 / 6227020800.0)
    for k in (-1.0 / 39916800.0, 1.0 / 362880.0, -1.0 / 5040.0, 1.0 / 120.0, -1.0 / 6.0):
        s = s * z + k
    c = jnp.full_like(z, -1.0 / 87178291200.0)
    for k in (1.0 / 479001600.0, -1.0 / 3628800.0, 1.0 / 40320.0, -1.0 / 720.0, 1.0 / 24.0, -0.5):
        c = c * z + k
    return x + x * (z * s), 1.0 + z * c


def resonance(detune, keep, lost, index):
    index = jnp.where(index > NT // 2, index - NT, index).astype(F32)
    s, c = sine_cosine_half((detune + index * STEP_HIGH) + index * STEP_LOW)
    re = lost + (2.0 * keep) * (s * s)
    im = (2.0 * keep) * (s * c)
    scale = 1.0 / (re * re + im * im)
    return re * scale, -(im * scale)


def cosine_sine(angle):
    s, c = sine_cosine_half(angle)
    return 1.0 - 2.0 * (s * s), 2.0 * (s * c)


def lost_by(rate):
    total = jnp.full_like(rate, 1.0 / 5040.0)
    for k in (-1.0 / 720.0, 1.0 / 120.0, -1.0 / 24.0, 1.0 / 6.0, -0.5, 1.0):
        total = k + rate * total
    return rate * total


def exact_dot(left, right):
    parts = thirds(left)
    return (dot(parts[0], right) + dot(parts[1], right)) + dot(parts[2], right)


def pick_dot(left, right):
    parts = thirds(right)
    return (dot(left, parts[0]) + dot(left, parts[1])) + dot(left, parts[2])


def pick_dot_nt(left, right):
    parts = thirds(right)
    return (dot_nt(left, parts[0]) + dot_nt(left, parts[1])) + dot_nt(left, parts[2])


def bin_columns(decay, detune):
    lost = lost_by(decay)
    keep = 1.0 - lost
    drive = jnp.sqrt(lost_by(2.0 * decay))
    cos, sin = cosine_sine(detune)
    p_re, p_im = keep * cos, -keep * sin
    whole = jnp.exp(-float(NT) * decay)
    far = float(NT) * detune
    turns = jnp.floor(far * (0.5 / math.pi) + 0.5)
    cos, sin = cosine_sine((far - turns * TURN[0]) - turns * TURN[1])
    r_re, r_im = 1.0 - whole * cos, whole * sin
    k_re, k_im = p_re * r_re - p_im * r_im, p_re * r_im + p_im * r_re
    rows = jnp.concatenate(
        [detune, keep, lost, drive, WEIGHT * k_im, -WEIGHT * k_re, keep, keep], 0
    )
    eye = (iota((BINS, BINS), 0) == iota((BINS, BINS), 1)).astype(BF16)
    return pick_dot_nt(eye, rows)


def pack(decay, detune, group_bin, spectral, lateral):
    row = [decay, detune, jnp.zeros((128 - 2 * BINS,), F32), group_bin.astype(F32)]
    return jnp.concatenate(row + [spectral, lateral]).reshape(42, 128)


def unpack(packed):
    return (packed[0:1, :BINS], packed[0:1, BINS : 2 * BINS], packed[1:2], packed[2:34],
            packed[34:42])


def couplings(drive, group_bin, occupation):
    member = (iota((BINS, GROUPS), 0).astype(F32) == group_bin).astype(BF16)
    return pick_dot_nt(member, occupation) * drive


def prepare_first(packed, occupation, quad):
    decay, detune_row, group_bin, spectral, _ = unpack(packed)
    params = bin_columns(decay, detune_row)
    detune, keep, lost, drive = (params[:, k : k + 1] for k in range(4))
    real, imag = [], []
    for w1 in range(16):
        g_re, g_im = resonance(detune, keep, lost, 16 * iota((BINS, 256), 1) + w1)
        real.append(g_re)
        imag.append(g_im)
    resonances = jnp.concatenate(halves(jnp.concatenate(real + imag, 0)), 0)
    per_bin = couplings(drive, group_bin, occupation)
    points = occupation.shape[0]
    pick = iota((points, 128), 0) == 4 * quad + iota((points, 128), 1) // 16 % 4
    chosen = exact_dot(per_bin, pick.astype(BF16))
    lane = iota((BINS, 128), 1)
    couple_row = jnp.sum(
        jnp.where(iota((BINS, 128), 0) == lane // 64 * 16 + lane % 16, chosen, 0.0),
        axis=0, keepdims=True,
    )
    cos, sin = cosine_sine(spectral)
    spectral_parts = cos, sin
    row_of = (iota((256, 32), 0) // 8 == iota((256, 32), 1)).astype(BF16)
    mine = iota((256, 128), 1) // 16 == iota((256, 128), 0) % 8
    lane_of = (iota((128, 128), 0) % 16 == iota((128, 128), 1) % 16).astype(BF16)
    cos = exact_dot(jnp.where(mine, pick_dot(row_of, cos), 0.0), lane_of)
    sin = exact_dot(jnp.where(mine, pick_dot(row_of, sin), 0.0), lane_of)
    side = jnp.where(iota((256, 128), 1) < 64, -1.0, 1.0)
    index = 16 * iota((256, 128), 0) + iota((256, 128), 1) % 16
    back_re, back_im = cosine_sine(jnp.where(index > NT // 2, NT - index, -index) * STEP)
    wrap_a = (cos * back_re - sin * back_im) * (1.0 / NT)
    wrap_b = (cos * back_im + sin * back_re) * (side * (1.0 / NT))
    first = jnp.concatenate([wrap_a, wrap_b, jnp.broadcast_to(couple_row, (8, 128))], 0)
    return resonances, first, params, per_bin, spectral_parts


def prepare_rest(packed, twiddle, made, here, quad):
    lateral = unpack(packed)[4]
    resonances, _, params, per_bin, (cos, sin) = made
    points = per_bin.shape[1]
    pick_rows = iota((64, points), 1) == 4 * quad + iota((64, points), 0) // 16
    spread = pick_dot_nt(pick_rows.astype(BF16), jnp.concatenate([per_bin] * 16, 0))
    couple_grid = jnp.where(
        iota((64, 512), 1) // 32 == iota((64, 512), 0) % 16, spread, 0.0
    )
    gain_high, gain_low = halves(couple_grid * WEIGHT)
    gain = dot(jnp.concatenate([gain_high, gain_low], 0),
               jnp.concatenate([resonances[:512], resonances[512:1024]], 1))
    gain_rest = dot(gain_high, jnp.concatenate([resonances[1024:1536], resonances[1536:]], 1))
    gain = (gain[:64] + gain[64:]) + gain_rest
    gain = jnp.concatenate([-gain[:, 256:], gain[:, :256]], 0)
    own = (iota((32, 128), 0) == here // 8) & (iota((32, 128), 1) // 16 == here % 8)
    lane_of = (iota((128, 128), 0) % 16 == iota((128, 128), 1) % 16).astype(BF16)
    own_rows = [jnp.sum(jnp.where(own, x, 0.0), axis=0, keepdims=True) for x in (cos, sin)]
    own_rows = exact_dot(jnp.concatenate(own_rows * 4, 0), lane_of)
    once_re, once_im = own_rows[0:1], own_rows[1:2]
    eye = (iota((128, 128), 0) == iota((128, 128), 1)).astype(BF16)
    cos, sin = cosine_sine(lateral)
    cos, sin = pick_dot_nt(eye, cos), pick_dot_nt(eye, sin)
    r, i = (
        [
            jnp.concatenate([x[:, 2 * k : 2 * k + 1], x[:, 2 * k + 1 : 2 * k + 2]], 0)
            for k in range(4)
        ]
        for x in (cos, sin)
    )
    blocks_re = [
        (r[0] + r[2]) + (r[1] + r[3]),
        (r[0] - r[2]) + (i[1] - i[3]),
        (r[0] + r[2]) - (r[1] + r[3]),
        (r[0] - r[2]) - (i[1] - i[3]),
    ]
    blocks_im = [
        (i[0] + i[2]) + (i[1] + i[3]),
        (i[0] - i[2]) - (r[1] - r[3]),
        (i[0] + i[2]) - (i[1] + i[3]),
        (i[0] - i[2]) + (r[1] - r[3]),
    ]
    eight = iota((256, 128), 1) // 16
    flip = jnp.where(eight < 4, -1.0, 1.0)
    mixing = [None] * 8
    for k in range(4):
        re, im = blocks_re[k] * (1.0 / NX), blocks_im[k] * (1.0 / NX)
        if k == 0:
            real, imag = re + jnp.zeros((256, 128), F32), im * flip
        else:
            cos, sin = twiddle[512 * k - 512 : 512 * k - 256], twiddle[512 * k - 256 : 512 * k]
            real, imag = cos * re - sin * im, (cos * im + sin * re) * flip
        for r in (k, k + 4):
            mixing[r] = jnp.where((eight + r) % 8 // 4 == eight // 4, real, imag)
    mixing = jnp.concatenate(mixing, 0)
    rows = jnp.concatenate([params[:16]] * 4 + [params[16:]] * 4, 0)
    g_re, g_im = resonance(
        rows[:, 0:1], rows[:, 1:2], rows[:, 2:3], 16 * here + iota((128, 128), 1) % 16
    )
    twice_re = once_re * once_re - once_im * once_im
    twice_im = 2.0 * once_re * once_im
    inside = iota((128, 128), 0) // 16 % 4 == iota((128, 128), 1) // 16 % 4
    left = iota((128, 128), 1) < 64
    f_re, f_im = -WEIGHT * twice_im, WEIGHT * twice_re
    b_re = jnp.where(inside, g_re * f_re - g_im * f_im, 0.0)
    b_im = jnp.where(inside, g_re * f_im + g_im * f_re, 0.0)
    gain_here = jnp.concatenate([b_re, jnp.where(left, -b_im, b_im)], 1)
    gain_here = jnp.concatenate(halves(gain_here), 0)
    side_row = jnp.where(iota((1, 128), 1) < 64, -1.0, 1.0)
    twice = jnp.concatenate([twice_re] * 8 + [twice_im * side_row] * 8, 0)
    k_re, k_im = rows[:, 4:5], rows[:, 5:6]
    f_re = once_re * k_re - once_im * k_im
    f_im = once_re * k_im + once_im * k_re
    h_re = jnp.where(inside, g_re * f_re - g_im * f_im, 0.0)
    h_im = jnp.where(inside, g_re * f_im + g_im * f_re, 0.0)
    top, bottom = jnp.where(left, h_re, h_im), jnp.where(left, -h_im, h_re)
    wrap_here = jnp.concatenate([top[:64], bottom[:64], top[64:], bottom[64:]], 0)
    wrap_here = jnp.concatenate(halves(wrap_here), 1)
    second = jnp.concatenate([twice, mixing], 0)
    second_tables = jnp.concatenate([gain_here, wrap_here], 0)
    turned = [jnp.broadcast_to(params[:, k : k + 1], (BINS, 128)) for k in (4, 5)]
    third = jnp.concatenate(
        [couple_grid[:, 128 * k : 128 * k + 128] for k in range(4)]
        + [gain[:, :128], gain[:, 128:]] + turned, 0,
    )
    return second, second_tables, third


def half_sign(shape):
    return jnp.where(iota(shape, 1) < 64, -1.0, 1.0)


def wrap_state(resonances, weighted, roll):
    product = dot(resonances, jnp.concatenate(halves(weighted), 1))
    product = quadrants(product, 1024, 128)
    lane = iota((BINS, 128), 1) % 16
    sums = []
    for part in range(2):
        total = jnp.zeros((BINS, 128), F32)
        for w1 in range(16):
            start = (part * 16 + w1) * BINS
            total = total + jnp.where(lane == w1, product[start : start + BINS], 0.0)
        sums.append(total)
    return sums[0] + half_sign((BINS, 128)) * roll(sums[1], 64)


def untwist(pair):
    return (jnp.concatenate([pair[k : k + 64], pair[128 + k : 192 + k]], 1) for k in (0, 64))


def to_rows(field, first, resonances, ahead, roll):
    mixed = table_times(ahead[:, 512:], field)
    mixed = jnp.concatenate([mixed[:128], mixed[128:]], 1)
    re, im = mixed[:64], mixed[64:]
    tc, ts = untwist(first)
    re, im = re * tc + im * ts, im * tc - re * ts
    both = jnp.concatenate(
        [jnp.concatenate([re, im], 1), jnp.concatenate([im, -re], 1)], 0
    )
    product = dot_nt(ahead[:, :512], jnp.concatenate(halves(both), 0))
    spectrum = quadrants(product, 256, 128)
    weighted = first[256:512] * spectrum + first[512:768] * roll(spectrum, 64)
    state = wrap_state(resonances[...], weighted, roll)
    place = (iota((128, 256), 0) // 16 == iota((128, 256), 1) % 128 // 16).astype(BF16)
    parts = exact_dot(state, place)
    lane = iota((BINS, 256), 1)
    chosen = iota((BINS, 256), 0) == lane // 128 * 16 + lane % 16
    state_row = jnp.sum(jnp.where(chosen, parts, 0.0), axis=0, keepdims=True)
    return spectrum, state_row[:, :128], state_row[:, 128:], first[768:769]


def diffract(blocks, wide, mixing, roll):
    sign = half_sign((256, 128))

    def transform(parts, direction):
        columns = []
        for part in parts:
            turned = roll(part, 64) * (sign * (-direction))
            columns += list(halves(jnp.concatenate([part, turned], 0)))
        product = dot(wide, jnp.concatenate(columns, 1))
        return [
            quadrants(product[:, 256 * k : 256 * k + 256], 256, 128) for k in range(len(parts))
        ]

    spectra = transform(blocks, 1.0)
    mixed = []
    for part in spectra:
        total = mixing[0] * part
        for r in range(1, 8):
            total = total + mixing[r] * roll(part, 128 - 16 * r)
        mixed.append(total)
    return transform(mixed, -1.0)


def columns_step(message, wide, second, second_tables, roll):
    field, state0, state1, couple = message
    mixing = [second[16 + 256 * k : 272 + 256 * k] for k in range(8)]
    field, state0, state1 = diffract([field, state0, state1], wide, mixing, roll)
    product = dot(jnp.concatenate(halves(couple), 0), second_tables[:128])
    rest = dot(couple.astype(BF16), second_tables[128:256])
    factor = (product[:256] + product[256:]) + rest
    turned = roll(couple, 64)
    left = iota((256, 128), 1) < 64
    states = jnp.concatenate(
        [state0 * jnp.where(left, couple, turned), state1 * jnp.where(left, turned, couple)], 1
    )
    wrapped = times_table(states, second_tables[256:])
    straight, crossed = factor[:, :128] + second[0:1], factor[:, 128:] + second[8:9]
    field = straight * field + crossed * roll(field, 64) + wrapped
    return diffract([field], wide, mixing, roll)[0]


def to_blocks(spectrum, resonances, third, back, shift, roll):
    sign = half_sign((256, 128))
    weighted = shift[:256] * spectrum + (shift[256:512] * sign) * roll(spectrum, 64)
    state = wrap_state(resonances[...], weighted, roll)
    state = third[512:544] * state + third[544:576] * (
        half_sign((BINS, 128)) * roll(state, 64)
    )
    gather = (iota((128, 128), 0) // 16 == iota((128, 128), 1) // 16).astype(BF16)
    spread = sum(dot_nt(gather, jnp.concatenate([part] * 16, 0)) for part in thirds(state))
    couple_grid = jnp.concatenate([third[64 * k : 64 * k + 64] for k in range(4)], 1)
    k_re, k_im = couple_grid * spread[:64], couple_grid * spread[64:]
    left = jnp.concatenate(
        [jnp.concatenate([k_re, -k_im], 1), jnp.concatenate([k_im, k_re], 1)], 0
    )
    left_high, left_low = halves(left)
    wrapped = dot(jnp.concatenate([left_high, left_low], 0), resonances[:1024])
    wrapped = (wrapped[:128] + wrapped[128:]) + dot(left_high, resonances[1024:])
    turned = spectrum.T
    re, im = turned[:64], turned[64:]
    gain = jnp.concatenate([third[256:384], third[384:512]], 1)
    gain_re, gain_im = gain[:64], gain[64:]
    out_re = re + (re * gain_re - im * gain_im) + wrapped[:64]
    out_im = im + (re * gain_im + im * gain_re) + wrapped[64:]
    both = jnp.concatenate(
        [jnp.concatenate([out_re, -out_im], 1), jnp.concatenate([out_im, out_re], 1)], 0
    )
    high, low = halves(both)
    mixed = dot(jnp.concatenate([high, low], 0), back[:512])
    mixed = (mixed[:128] + mixed[128:]) + dot(high, back[512:1024])
    re, im = mixed[:64], mixed[64:]
    tc, ts = untwist(shift[512:])
    re, im = re * tc - im * ts, im * tc + re * ts
    mixed = jnp.concatenate(
        [re[:, :128], im[:, :128], re[:, 128:], im[:, 128:]], 0
    ) * (1.0 / NT)
    return table_times(back[1024:], mixed)


def lane_roll(value, shift):
    return pltpu.roll(value, shift, 1)


def shape(*dims, dtype=F32):
    return jax.ShapeDtypeStruct(dims, dtype)


VMEM_SPEC = pl.BlockSpec(memory_space=pltpu.VMEM)
HBM_SPEC = pl.BlockSpec(memory_space=pltpu.HBM)


def call(kernel, out_shape, in_specs, out_specs, scratch, *operands, flops, limit=40):
    moved = sum(x.size * x.dtype.itemsize for x in operands)
    return pl.pallas_call(
        kernel,
        out_shape=out_shape,
        in_specs=in_specs,
        out_specs=out_specs,
        scratch_shapes=scratch,
        compiler_params=pltpu.CompilerParams(vmem_limit_bytes=limit * 1024 * 1024),
        cost_estimate=pl.CostEstimate(flops=flops, bytes_accessed=moved, transcendentals=0),
    )(*operands)


def halves_of_tiles(upper, lower):
    low = iota((8, 128), 0) < 4
    return (
        jnp.where(low, upper, pltpu.roll(lower, 4, 0)),
        jnp.where(low, pltpu.roll(upper, 4, 0), lower),
    )


def cut_kernel(field, out):
    for c in range(2):
        for row in range(8):
            tile = field[c, 8 * row : 8 * row + 8, :]
            first, second = halves_of_tiles(tile[:, :128], tile[:, 128:])
            out[32 * row + 8 * c : 32 * row + 8 * c + 8, :] = first
            out[32 * row + 16 + 8 * c : 32 * row + 24 + 8 * c, :] = second


def join_kernel(rows, field, buffer, sems):
    copies = []
    for c in range(2):
        for row in range(8):
            first = rows[32 * row + 8 * c : 32 * row + 8 * c + 8, :]
            second = rows[32 * row + 16 + 8 * c : 32 * row + 24 + 8 * c, :]
            upper, lower = halves_of_tiles(first, second)
            buffer[c, 8 * row : 8 * row + 8, :128] = upper
            buffer[c, 8 * row : 8 * row + 8, 128:] = lower
        copies.append(pltpu.make_async_copy(buffer.at[c], field.at[c], sems.at[c]))
        copies[-1].start()
    for copy in copies:
        copy.wait()


PREPARED = (
    shape(2048, 256, dtype=BF16), shape(776, 128), shape(2064, 128), shape(512, 256, dtype=BF16),
    shape(576, 128),
)


def prepare_kernel(packed, occupation, twiddle, *outs):
    quad = lax.axis_index("tm")
    here = lax.axis_index("lat") * 16 + quad
    packed = packed[...]
    made = prepare_first(packed, occupation[...], quad)
    first = jnp.concatenate([twiddle[1536:], made[1]], 0)
    values = (made[0], first, *prepare_rest(packed, twiddle, made, here, quad))
    for ref, value in zip(outs, values):
        ref[...] = value


def rows_kernel(field, first, resonances, ahead, out):
    spectrum, *rest = to_rows(field[...], first, resonances, ahead, lane_roll)
    out[pl.ds(0, 256, stride=4), :] = spectrum
    for k, row in enumerate(rest):
        out[pl.ds(k + 1, 256, stride=4), :] = jnp.broadcast_to(row, (256, 128))


def columns_kernel(message, ahead, second, second_tables, out):
    parts = [message[pl.ds(k, 256, stride=4), :] for k in range(4)]
    out[...] = columns_step(parts, ahead[:, :512], second, second_tables[...], lane_roll)


def blocks_kernel(spectrum, resonances, third, back, shift, out):
    out[...] = to_blocks(
        spectrum[...], resonances[...], third[...], back[...], shift[...], lane_roll
    )


def on_device(
    light_field, lateral_phase, spectral_phase, occupation, bin_decay, bin_detune, group_bin
):
    t = {name: jnp.asarray(value) for name, value in TABLES.items()}
    sems = pltpu.SemaphoreType.DMA
    rows = call(
        cut_kernel, shape(256, 128), [VMEM_SPEC], VMEM_SPEC, [], light_field, flops=1000
    )
    rows = lax.all_to_all(rows.reshape(16, 16, 128), "tm", 0, 0, tiled=True)
    packed = pack(bin_decay, bin_detune, group_bin, spectral_phase, lateral_phase)
    resonances, first, second, second_tables, third = call(
        prepare_kernel, PREPARED, [VMEM_SPEC] * 3, (VMEM_SPEC,) * 5, [],
        packed, occupation.T, t["twiddle"], flops=200_000_000,
    )
    message = call(
        rows_kernel, shape(1024, 128), [VMEM_SPEC] * 4, VMEM_SPEC, [],
        rows.reshape(256, 128), first, resonances, t["ahead"],
        flops=500_000_000,
    )
    message = lax.all_to_all(message.reshape(256, 4, 128), BOTH, 0, 0, tiled=True)
    columns = call(
        columns_kernel, shape(256, 128), [VMEM_SPEC] * 4, VMEM_SPEC, [],
        message.reshape(1024, 128), t["ahead"], second, second_tables, flops=1_000_000_000,
    )
    spectrum = lax.all_to_all(columns, BOTH, 0, 0, tiled=True)
    finished = call(
        blocks_kernel, shape(256, 128), [VMEM_SPEC] * 5, VMEM_SPEC, [],
        spectrum, resonances, third, t["back"], t["shift"], flops=800_000_000,
    )
    turned = lax.all_to_all(finished.reshape(16, 16, 128), "tm", 0, 0, tiled=True)
    return call(
        join_kernel, shape(2, 64, 256), [VMEM_SPEC], HBM_SPEC,
        [pltpu.VMEM((2, 64, 256), F32), sems((2,))], turned.reshape(256, 128), flops=1000,
    )


def solution(mesh):
    return jax.shard_map(
        on_device,
        mesh=mesh,
        in_specs=(P(None, "lat", "tm"), P(), P(), P(None, "lat"), P(), P(), P()),
        out_specs=P(None, "lat", "tm"),
        check_vma=False,
    )
```

```python
import math

import jax
import jax.numpy as jnp
import numpy as np
from jax import lax
from jax.experimental import pallas as pl
from jax.experimental.pallas import tpu as pltpu
from jax.sharding import PartitionSpec as P

NX, NT, BINS, GROUPS = 1024, 4096, 32, 128
WEIGHT = 0.5 / math.sqrt(GROUPS)
F32, BF16 = jnp.float32, jnp.bfloat16
BOTH = ("lat", "tm")


def split_table(table):
    high = table.astype(np.float32).astype(jnp.bfloat16)
    low = (table - high.astype(np.float64)).astype(jnp.bfloat16)
    return high, low


def build_tables():
    grid = np.arange
    angle = 2 * np.pi * (grid(256)[:, None] * grid(256)[None, :] % 256) / 256
    wide = np.concatenate([np.cos(angle), np.sin(angle)], 1)
    tall = np.concatenate([np.cos(angle), np.sin(angle)], 0)
    lane = grid(128)
    c, q, col = lane // 64, lane // 16 % 4, lane % 16
    to, row = grid(256), grid(256)
    th, tc, tq, tw = to // 128, to // 64 % 2, to // 16 % 4, to % 16
    rm, rc, rh, rq = row // 16, row // 8 % 2, row // 4 % 2, row % 4
    turn = 2 * np.pi * (tw[:, None] * rm[None, :] % 16) / 16
    sign = np.where(tc[:, None] == 0, 1.0, -1.0)
    small = np.where(tc[:, None] == rc[None, :], np.cos(turn), sign * np.sin(turn))
    small = small * (tq[:, None] == rq[None, :]) * (th[:, None] == rh[None, :])
    short = 2 * np.pi * (col[:64, None] * grid(256)[None, :]) / NT
    omega_lanes = np.tile(2 * np.pi * (16 * grid(256)[:, None] + grid(16)[None, :]) / NT, (1, 8))
    t = {}
    t["ahead"] = np.concatenate(
        [np.concatenate(split_table(x), 0) for x in (wide, small)], 1
    )
    t["back"] = np.concatenate(split_table(tall) + split_table(small.T), 0)
    twist = np.concatenate([np.cos(short), np.sin(short)], 0)
    omega_part = np.concatenate([np.cos(omega_lanes), -np.sin(omega_lanes)], 0)
    twist = [twist[:, :128], twist[:, 128:]]
    t["shift"] = np.concatenate([omega_part / NT] + twist, 0).astype(np.float32)
    return t


STEP = 2 * math.pi / NT
STEP_HIGH = round(STEP * 2**22) / 2**22
STEP_LOW = STEP - STEP_HIGH
TURN = (6.28125, 2 * math.pi - 6.28125)
TABLES = build_tables()


def iota(shape, dim):
    return lax.broadcasted_iota(jnp.int32, shape, dim)


def halves(value):
    high = value.astype(BF16)
    return high, (value - high.astype(F32)).astype(BF16)


def thirds(value):
    high = value.astype(BF16)
    rest = value - high.astype(F32)
    middle = rest.astype(BF16)
    return high, middle, (rest - middle.astype(F32)).astype(BF16)


def dot(left, right):
    return lax.dot_general(left, right, (((1,), (0,)), ((), ())), preferred_element_type=F32)


def dot_nt(left, right):
    return lax.dot_general(left, right, (((1,), (1,)), ((), ())), preferred_element_type=F32)


def quadrants(product, rows, cols):
    return product[:rows, :cols] + (product[:rows, cols:] + product[rows:, :cols])


def table_times(table, value):
    product = dot(table, jnp.concatenate(halves(value), 1))
    return quadrants(product, table.shape[0] // 2, value.shape[1])


def times_table(value, table):
    product = dot(jnp.concatenate(halves(value), 0), table)
    return quadrants(product, value.shape[0], table.shape[1] // 2)


def sine_cosine_half(angle):
    x = angle * 0.5
    z = x * x
    s = jnp.full_like(z, 1.0 / 6227020800.0)
    for k in (-1.0 / 39916800.0, 1.0 / 362880.0, -1.0 / 5040.0, 1.0 / 120.0, -1.0 / 6.0):
        s = s * z + k
    c = jnp.full_like(z, -1.0 / 87178291200.0)
    for k in (1.0 / 479001600.0, -1.0 / 3628800.0, 1.0 / 40320.0, -1.0 / 720.0, 1.0 / 24.0, -0.5):
        c = c * z + k
    return x + x * (z * s), 1.0 + z * c


def resonance(detune, keep, lost, index):
    index = jnp.where(index > NT // 2, index - NT, index).astype(F32)
    s, c = sine_cosine_half((detune + index * STEP_HIGH) + index * STEP_LOW)
    re = lost + (2.0 * keep) * (s * s)
    im = (2.0 * keep) * (s * c)
    scale = 1.0 / (re * re + im * im)
    return re * scale, -(im * scale)


def cosine_sine(angle):
    s, c = sine_cosine_half(angle)
    return 1.0 - 2.0 * (s * s), 2.0 * (s * c)


def lost_by(rate):
    total = jnp.full_like(rate, 1.0 / 5040.0)
    for k in (-1.0 / 720.0, 1.0 / 120.0, -1.0 / 24.0, 1.0 / 6.0, -0.5, 1.0):
        total = k + rate * total
    return rate * total


def exact_dot(left, right):
    parts = thirds(left)
    return (dot(parts[0], right) + dot(parts[1], right)) + dot(parts[2], right)


def pick_dot(left, right):
    parts = thirds(right)
    return (dot(left, parts[0]) + dot(left, parts[1])) + dot(left, parts[2])


def pick_dot_nt(left, right):
    parts = thirds(right)
    return (dot_nt(left, parts[0]) + dot_nt(left, parts[1])) + dot_nt(left, parts[2])


def bin_columns(decay, detune):
    lost = lost_by(decay)
    keep = 1.0 - lost
    drive = jnp.sqrt(lost_by(2.0 * decay))
    cos, sin = cosine_sine(detune)
    p_re, p_im = keep * cos, -keep * sin
    whole = jnp.exp(-float(NT) * decay)
    far = float(NT) * detune
    turns = jnp.floor(far * (0.5 / math.pi) + 0.5)
    cos, sin = cosine_sine((far - turns * TURN[0]) - turns * TURN[1])
    r_re, r_im = 1.0 - whole * cos, whole * sin
    k_re, k_im = p_re * r_re - p_im * r_im, p_re * r_im + p_im * r_re
    rows = jnp.concatenate(
        [detune, keep, lost, drive, WEIGHT * k_im, -WEIGHT * k_re, keep, keep], 0
    )
    eye = (iota((BINS, BINS), 0) == iota((BINS, BINS), 1)).astype(BF16)
    return pick_dot_nt(eye, rows)


def pack(decay, detune, group_bin, spectral, lateral, occupation):
    parts = [decay, detune, group_bin.astype(F32), spectral, lateral, occupation.T.reshape(-1)]
    starts = [0, BINS, 128, 256, 256 + NT, 256 + NT + NX]
    total = starts[-1] + parts[-1].size
    padded = [
        jnp.pad(part, (start, total - start - part.size)) for part, start in zip(parts, starts)
    ]
    return sum(padded[1:], padded[0]).reshape(total // 128, 128)


def unpack(packed):
    return (packed[0:1, :BINS], packed[0:1, BINS : 2 * BINS], packed[1:2], packed[2:34],
            packed[34:42], packed[42:])


def couplings(drive, group_bin, occupation):
    member = (iota((BINS, GROUPS), 0).astype(F32) == group_bin).astype(BF16)
    return pick_dot_nt(member, occupation) * drive


def prepare_first(packed, quad):
    decay, detune_row, group_bin, spectral, _, occupation = unpack(packed)
    params = bin_columns(decay, detune_row)
    detune, keep, lost, drive = (params[:, k : k + 1] for k in range(4))
    real, imag = [], []
    for w1 in range(16):
        g_re, g_im = resonance(detune, keep, lost, 16 * iota((BINS, 256), 1) + w1)
        real.append(g_re)
        imag.append(g_im)
    resonances = jnp.concatenate(halves(jnp.concatenate(real + imag, 0)), 0)
    per_bin = couplings(drive, group_bin, occupation)
    points = occupation.shape[0]
    pick = iota((points, 128), 0) == 4 * quad + iota((points, 128), 1) // 16 % 4
    chosen = exact_dot(per_bin, pick.astype(BF16))
    lane = iota((BINS, 128), 1)
    couple_row = jnp.sum(
        jnp.where(iota((BINS, 128), 0) == lane // 64 * 16 + lane % 16, chosen, 0.0),
        axis=0, keepdims=True,
    )
    cos, sin = cosine_sine(spectral)
    spectral_parts = cos, sin
    row_of = (iota((256, 32), 0) // 8 == iota((256, 32), 1)).astype(BF16)
    mine = iota((256, 128), 1) // 16 == iota((256, 128), 0) % 8
    lane_of = (iota((128, 128), 0) % 16 == iota((128, 128), 1) % 16).astype(BF16)
    cos = exact_dot(jnp.where(mine, pick_dot(row_of, cos), 0.0), lane_of)
    sin = exact_dot(jnp.where(mine, pick_dot(row_of, sin), 0.0), lane_of)
    side = jnp.where(iota((256, 128), 1) < 64, -1.0, 1.0)
    index = 16 * iota((256, 128), 0) + iota((256, 128), 1) % 16
    back_re, back_im = cosine_sine(jnp.where(index > NT // 2, NT - index, -index) * STEP)
    wrap_a = (cos * back_re - sin * back_im) * (1.0 / NT)
    wrap_b = (cos * back_im + sin * back_re) * (side * (1.0 / NT))
    index = (iota((64, 256), 0) % 16) * iota((64, 256), 1)
    tc, ts = cosine_sine(jnp.where(index > NT // 2, index - NT, index).astype(F32) * STEP)
    first = jnp.concatenate(
        [tc[:, :128], ts[:, :128], tc[:, 128:], ts[:, 128:], wrap_a, wrap_b,
         jnp.broadcast_to(couple_row, (8, 128))],
        0,
    )
    return resonances, first, params, per_bin, spectral_parts


def prepare_rest(packed, made, here, quad):
    lateral = unpack(packed)[4]
    resonances, _, params, per_bin, (cos, sin) = made
    points = per_bin.shape[1]
    pick_rows = iota((64, points), 1) == 4 * quad + iota((64, points), 0) // 16
    spread = pick_dot_nt(pick_rows.astype(BF16), jnp.concatenate([per_bin] * 16, 0))
    couple_grid = jnp.where(
        iota((64, 512), 1) // 32 == iota((64, 512), 0) % 16, spread, 0.0
    )
    gain_high, gain_low = halves(couple_grid * WEIGHT)
    gain = dot(jnp.concatenate([gain_high, gain_low], 0),
               jnp.concatenate([resonances[:512], resonances[512:1024]], 1))
    gain_rest = dot(gain_high, jnp.concatenate([resonances[1024:1536], resonances[1536:]], 1))
    gain = (gain[:64] + gain[64:]) + gain_rest
    gain = jnp.concatenate([-gain[:, 256:], gain[:, :256]], 0)
    own = (iota((32, 128), 0) == here // 8) & (iota((32, 128), 1) // 16 == here % 8)
    lane_of = (iota((128, 128), 0) % 16 == iota((128, 128), 1) % 16).astype(BF16)
    own_rows = [jnp.sum(jnp.where(own, x, 0.0), axis=0, keepdims=True) for x in (cos, sin)]
    own_rows = exact_dot(jnp.concatenate(own_rows * 4, 0), lane_of)
    once_re, once_im = own_rows[0:1], own_rows[1:2]
    eye = (iota((128, 128), 0) == iota((128, 128), 1)).astype(BF16)
    cos, sin = cosine_sine(lateral)
    cos, sin = pick_dot_nt(eye, cos), pick_dot_nt(eye, sin)
    r, i = (
        [
            jnp.concatenate([x[:, 2 * k : 2 * k + 1], x[:, 2 * k + 1 : 2 * k + 2]], 0)
            for k in range(4)
        ]
        for x in (cos, sin)
    )
    blocks_re = [
        (r[0] + r[2]) + (r[1] + r[3]),
        (r[0] - r[2]) + (i[1] - i[3]),
        (r[0] + r[2]) - (r[1] + r[3]),
        (r[0] - r[2]) - (i[1] - i[3]),
    ]
    blocks_im = [
        (i[0] + i[2]) + (i[1] + i[3]),
        (i[0] - i[2]) - (r[1] - r[3]),
        (i[0] + i[2]) - (i[1] + i[3]),
        (i[0] - i[2]) + (r[1] - r[3]),
    ]
    eight = iota((256, 128), 1) // 16
    flip = jnp.where(eight < 4, -1.0, 1.0)
    index = iota((256, 128), 0)
    cos1, sin1 = cosine_sine(index.astype(F32) * (-2.0 * math.pi / NX))
    cos2, sin2 = cos1 * cos1 - sin1 * sin1, 2.0 * (cos1 * sin1)
    cos3, sin3 = cos1 * cos2 - sin1 * sin2, cos1 * sin2 + sin1 * cos2
    turns = [None, (cos1, sin1), (cos2, sin2), (cos3, sin3)]
    mixing = [None] * 8
    for k in range(4):
        re, im = blocks_re[k] * (1.0 / NX), blocks_im[k] * (1.0 / NX)
        if k == 0:
            real, imag = re + jnp.zeros((256, 128), F32), im * flip
        else:
            near = eight % 4 + k < 4
            cos = jnp.where(near, turns[k][0], turns[4 - k][0])
            sin = jnp.where(near, turns[k][1], -turns[4 - k][1])
            real, imag = cos * re - sin * im, (cos * im + sin * re) * flip
        for r in (k, k + 4):
            mixing[r] = jnp.where((eight + r) % 8 // 4 == eight // 4, real, imag)
    mixing = jnp.concatenate(mixing, 0)
    rows = jnp.concatenate([params[:16]] * 4 + [params[16:]] * 4, 0)
    g_re, g_im = resonance(
        rows[:, 0:1], rows[:, 1:2], rows[:, 2:3], 16 * here + iota((128, 128), 1) % 16
    )
    twice_re = once_re * once_re - once_im * once_im
    twice_im = 2.0 * once_re * once_im
    inside = iota((128, 128), 0) // 16 % 4 == iota((128, 128), 1) // 16 % 4
    left = iota((128, 128), 1) < 64
    f_re, f_im = -WEIGHT * twice_im, WEIGHT * twice_re
    b_re = jnp.where(inside, g_re * f_re - g_im * f_im, 0.0)
    b_im = jnp.where(inside, g_re * f_im + g_im * f_re, 0.0)
    gain_here = jnp.concatenate([b_re, jnp.where(left, -b_im, b_im)], 1)
    gain_here = jnp.concatenate(halves(gain_here), 0)
    side_row = jnp.where(iota((1, 128), 1) < 64, -1.0, 1.0)
    twice = jnp.concatenate([twice_re] * 8 + [twice_im * side_row] * 8, 0)
    k_re, k_im = rows[:, 4:5], rows[:, 5:6]
    f_re = once_re * k_re - once_im * k_im
    f_im = once_re * k_im + once_im * k_re
    h_re = jnp.where(inside, g_re * f_re - g_im * f_im, 0.0)
    h_im = jnp.where(inside, g_re * f_im + g_im * f_re, 0.0)
    top, bottom = jnp.where(left, h_re, h_im), jnp.where(left, -h_im, h_re)
    wrap_here = jnp.concatenate([top[:64], bottom[:64], top[64:], bottom[64:]], 0)
    wrap_here = jnp.concatenate(halves(wrap_here), 1)
    second = jnp.concatenate([twice, mixing], 0)
    second_tables = jnp.concatenate([gain_here, wrap_here], 0)
    turned = [jnp.broadcast_to(params[:, k : k + 1], (BINS, 128)) for k in (4, 5)]
    third = jnp.concatenate(
        [couple_grid[:, 128 * k : 128 * k + 128] for k in range(4)]
        + [gain[:, :128], gain[:, 128:]] + turned, 0,
    )
    return second, second_tables, third


def half_sign(shape):
    return jnp.where(iota(shape, 1) < 64, -1.0, 1.0)


def wrap_state(resonances, weighted, roll):
    product = dot(resonances, jnp.concatenate(halves(weighted), 1))
    product = quadrants(product, 1024, 128)
    lane = iota((BINS, 128), 1) % 16
    sums = []
    for part in range(2):
        total = jnp.zeros((BINS, 128), F32)
        for w1 in range(16):
            start = (part * 16 + w1) * BINS
            total = total + jnp.where(lane == w1, product[start : start + BINS], 0.0)
        sums.append(total)
    return sums[0] + half_sign((BINS, 128)) * roll(sums[1], 64)


def untwist(pair):
    return (jnp.concatenate([pair[k : k + 64], pair[128 + k : 192 + k]], 1) for k in (0, 64))


def to_rows(field, first, resonances, ahead, roll):
    mixed = table_times(ahead[:, 512:], field)
    mixed = jnp.concatenate([mixed[:128], mixed[128:]], 1)
    re, im = mixed[:64], mixed[64:]
    tc, ts = untwist(first)
    re, im = re * tc + im * ts, im * tc - re * ts
    both = jnp.concatenate(
        [jnp.concatenate([re, im], 1), jnp.concatenate([im, -re], 1)], 0
    )
    product = dot_nt(ahead[:, :512], jnp.concatenate(halves(both), 0))
    spectrum = quadrants(product, 256, 128)
    weighted = first[256:512] * spectrum + first[512:768] * roll(spectrum, 64)
    state = wrap_state(resonances[...], weighted, roll)
    place = (iota((128, 256), 0) // 16 == iota((128, 256), 1) % 128 // 16).astype(BF16)
    parts = exact_dot(state, place)
    lane = iota((BINS, 256), 1)
    chosen = iota((BINS, 256), 0) == lane // 128 * 16 + lane % 16
    state_row = jnp.sum(jnp.where(chosen, parts, 0.0), axis=0, keepdims=True)
    return spectrum, state_row[:, :128], state_row[:, 128:], first[768:769]


def diffract(blocks, wide, mixing, roll):
    sign = half_sign((256, 128))

    def transform(parts, direction):
        columns = []
        for part in parts:
            turned = roll(part, 64) * (sign * (-direction))
            columns += list(halves(jnp.concatenate([part, turned], 0)))
        product = dot(wide, jnp.concatenate(columns, 1))
        return [
            quadrants(product[:, 256 * k : 256 * k + 256], 256, 128) for k in range(len(parts))
        ]

    spectra = transform(blocks, 1.0)
    mixed = []
    for part in spectra:
        total = mixing[0] * part
        for r in range(1, 8):
            total = total + mixing[r] * roll(part, 128 - 16 * r)
        mixed.append(total)
    return transform(mixed, -1.0)


def columns_step(message, wide, second, second_tables, roll):
    field, state0, state1, couple = message
    mixing = [second[16 + 256 * k : 272 + 256 * k] for k in range(8)]
    field, state0, state1 = diffract([field, state0, state1], wide, mixing, roll)
    product = dot(jnp.concatenate(halves(couple), 0), second_tables[:128])
    rest = dot(couple.astype(BF16), second_tables[128:256])
    factor = (product[:256] + product[256:]) + rest
    turned = roll(couple, 64)
    left = iota((256, 128), 1) < 64
    states = jnp.concatenate(
        [state0 * jnp.where(left, couple, turned), state1 * jnp.where(left, turned, couple)], 1
    )
    wrapped = times_table(states, second_tables[256:])
    straight, crossed = factor[:, :128] + second[0:1], factor[:, 128:] + second[8:9]
    field = straight * field + crossed * roll(field, 64) + wrapped
    return diffract([field], wide, mixing, roll)[0]


def to_blocks(spectrum, resonances, third, back, shift, roll):
    sign = half_sign((256, 128))
    weighted = shift[:256] * spectrum + (shift[256:512] * sign) * roll(spectrum, 64)
    state = wrap_state(resonances[...], weighted, roll)
    state = third[512:544] * state + third[544:576] * (
        half_sign((BINS, 128)) * roll(state, 64)
    )
    gather = (iota((128, 128), 0) // 16 == iota((128, 128), 1) // 16).astype(BF16)
    spread = sum(dot_nt(gather, jnp.concatenate([part] * 16, 0)) for part in thirds(state))
    couple_grid = jnp.concatenate([third[64 * k : 64 * k + 64] for k in range(4)], 1)
    k_re, k_im = couple_grid * spread[:64], couple_grid * spread[64:]
    left = jnp.concatenate(
        [jnp.concatenate([k_re, -k_im], 1), jnp.concatenate([k_im, k_re], 1)], 0
    )
    left_high, left_low = halves(left)
    wrapped = dot(jnp.concatenate([left_high, left_low], 0), resonances[:1024])
    wrapped = (wrapped[:128] + wrapped[128:]) + dot(left_high, resonances[1024:])
    turned = spectrum.T
    re, im = turned[:64], turned[64:]
    gain = jnp.concatenate([third[256:384], third[384:512]], 1)
    gain_re, gain_im = gain[:64], gain[64:]
    out_re = re + (re * gain_re - im * gain_im) + wrapped[:64]
    out_im = im + (re * gain_im + im * gain_re) + wrapped[64:]
    both = jnp.concatenate(
        [jnp.concatenate([out_re, -out_im], 1), jnp.concatenate([out_im, out_re], 1)], 0
    )
    high, low = halves(both)
    mixed = dot(jnp.concatenate([high, low], 0), back[:512])
    mixed = (mixed[:128] + mixed[128:]) + dot(high, back[512:1024])
    re, im = mixed[:64], mixed[64:]
    tc, ts = untwist(shift[512:])
    re, im = re * tc - im * ts, im * tc + re * ts
    mixed = jnp.concatenate(
        [re[:, :128], im[:, :128], re[:, 128:], im[:, 128:]], 0
    ) * (1.0 / NT)
    return table_times(back[1024:], mixed)


def lane_roll(value, shift):
    return pltpu.roll(value, shift, 1)


def shape(*dims, dtype=F32):
    return jax.ShapeDtypeStruct(dims, dtype)


VMEM_SPEC = pl.BlockSpec(memory_space=pltpu.VMEM)
HBM_SPEC = pl.BlockSpec(memory_space=pltpu.HBM)


def call(kernel, out_shape, in_specs, out_specs, scratch, *operands, flops, limit=40):
    moved = sum(x.size * x.dtype.itemsize for x in operands)
    return pl.pallas_call(
        kernel,
        out_shape=out_shape,
        in_specs=in_specs,
        out_specs=out_specs,
        scratch_shapes=scratch,
        compiler_params=pltpu.CompilerParams(vmem_limit_bytes=limit * 1024 * 1024),
        cost_estimate=pl.CostEstimate(flops=flops, bytes_accessed=moved, transcendentals=0),
    )(*operands)


def halves_of_tiles(upper, lower):
    low = iota((8, 128), 0) < 4
    return (
        jnp.where(low, upper, pltpu.roll(lower, 4, 0)),
        jnp.where(low, pltpu.roll(upper, 4, 0), lower),
    )


def cut_kernel(field, out):
    for c in range(2):
        for row in range(8):
            tile = field[c, 8 * row : 8 * row + 8, :]
            first, second = halves_of_tiles(tile[:, :128], tile[:, 128:])
            out[32 * row + 8 * c : 32 * row + 8 * c + 8, :] = first
            out[32 * row + 16 + 8 * c : 32 * row + 24 + 8 * c, :] = second


def join_kernel(rows, field, buffer, sems):
    copies = []
    for c in range(2):
        for row in range(8):
            first = rows[32 * row + 8 * c : 32 * row + 8 * c + 8, :]
            second = rows[32 * row + 16 + 8 * c : 32 * row + 24 + 8 * c, :]
            upper, lower = halves_of_tiles(first, second)
            buffer[c, 8 * row : 8 * row + 8, :128] = upper
            buffer[c, 8 * row : 8 * row + 8, 128:] = lower
        copies.append(pltpu.make_async_copy(buffer.at[c], field.at[c], sems.at[c]))
        copies[-1].start()
    for copy in copies:
        copy.wait()


PREPARED = (shape(2560, 256, dtype=BF16), shape(3416, 128))


def prepare_kernel(packed, ahead, tables, later):
    quad = lax.axis_index("tm")
    here = lax.axis_index("lat") * 16 + quad
    packed = packed[...]
    made = prepare_first(packed, quad)
    second, second_tables, third = prepare_rest(packed, made, here, quad)
    tables[:2048] = made[0]
    tables[2048:] = second_tables
    later[:2064] = second
    later[2064:2640] = third
    later[2640:] = made[1]


def rows_kernel(field, tables, later, ahead, out):
    spectrum, *rest = to_rows(
        field[...], later[2640:], tables.at[:2048], ahead, lane_roll
    )
    out[pl.ds(0, 256, stride=4), :] = spectrum
    for k, row in enumerate(rest):
        out[pl.ds(k + 1, 256, stride=4), :] = jnp.broadcast_to(row, (256, 128))


def columns_kernel(message, ahead, tables, later, out):
    parts = [message[pl.ds(k, 256, stride=4), :] for k in range(4)]
    out[...] = columns_step(parts, ahead[:, :512], later, tables[2048:], lane_roll)


def blocks_kernel(spectrum, tables, later, back, shift, out):
    out[...] = to_blocks(
        spectrum[...], tables[:2048], later[2064:2640], back[...], shift[...], lane_roll
    )


def on_device(
    light_field, lateral_phase, spectral_phase, occupation, bin_decay, bin_detune, group_bin
):
    t = {name: jnp.asarray(value) for name, value in TABLES.items()}
    sems = pltpu.SemaphoreType.DMA
    rows = call(
        cut_kernel, shape(256, 128), [VMEM_SPEC], VMEM_SPEC, [], light_field, flops=1000
    )
    rows = lax.all_to_all(rows.reshape(16, 16, 128), "tm", 0, 0, tiled=True)
    packed = pack(
        bin_decay, bin_detune, group_bin, spectral_phase, lateral_phase, occupation
    )
    tables, later = call(
        prepare_kernel, PREPARED, [VMEM_SPEC] * 2, (VMEM_SPEC,) * 2, [], packed, t["ahead"],
        flops=200_000_000,
    )
    message = call(
        rows_kernel, shape(1024, 128), [VMEM_SPEC] * 4, VMEM_SPEC, [],
        rows.reshape(256, 128), tables, later, t["ahead"],
        flops=500_000_000,
    )
    message = lax.all_to_all(message.reshape(256, 4, 128), BOTH, 0, 0, tiled=True)
    columns = call(
        columns_kernel, shape(256, 128), [VMEM_SPEC] * 4, VMEM_SPEC, [],
        message.reshape(1024, 128), t["ahead"], tables, later, flops=1_000_000_000,
    )
    spectrum = lax.all_to_all(columns, BOTH, 0, 0, tiled=True)
    finished = call(
        blocks_kernel, shape(256, 128), [VMEM_SPEC] * 5, VMEM_SPEC, [],
        spectrum, tables, later, t["back"], t["shift"], flops=800_000_000,
    )
    turned = lax.all_to_all(finished.reshape(16, 16, 128), "tm", 0, 0, tiled=True)
    return call(
        join_kernel, shape(2, 64, 256), [VMEM_SPEC], HBM_SPEC,
        [pltpu.VMEM((2, 64, 256), F32), sems((2,))], turned.reshape(256, 128), flops=1000,
    )


def solution(mesh):
    return jax.shard_map(
        on_device,
        mesh=mesh,
        in_specs=(P(None, "lat", "tm"), P(), P(), P(None, "lat"), P(), P(), P()),
        out_specs=P(None, "lat", "tm"),
        check_vma=False,
    )
```

```python
import math

import jax
import jax.numpy as jnp
import numpy as np
from jax import lax
from jax.experimental import pallas as pl
from jax.experimental.pallas import tpu as pltpu
from jax.sharding import PartitionSpec as P

NX, NT, BINS, GROUPS = 1024, 4096, 32, 128
WEIGHT = 0.5 / math.sqrt(GROUPS)
F32, BF16 = jnp.float32, jnp.bfloat16
BOTH = ("lat", "tm")


def split_table(table):
    high = table.astype(np.float32).astype(jnp.bfloat16)
    low = (table - high.astype(np.float64)).astype(jnp.bfloat16)
    return high, low


def build_tables():
    grid = np.arange
    angle = 2 * np.pi * (grid(256)[:, None] * grid(256)[None, :] % 256) / 256
    wide = np.concatenate([np.cos(angle), np.sin(angle)], 1)
    tall = np.concatenate([np.cos(angle), np.sin(angle)], 0)
    lane = grid(128)
    c, q, col = lane // 64, lane // 16 % 4, lane % 16
    to, row = grid(256), grid(256)
    th, tc, tq, tw = to // 128, to // 64 % 2, to // 16 % 4, to % 16
    rm, rc, rh, rq = row // 16, row // 8 % 2, row // 4 % 2, row % 4
    turn = 2 * np.pi * (tw[:, None] * rm[None, :] % 16) / 16
    sign = np.where(tc[:, None] == 0, 1.0, -1.0)
    small = np.where(tc[:, None] == rc[None, :], np.cos(turn), sign * np.sin(turn))
    small = small * (tq[:, None] == rq[None, :]) * (th[:, None] == rh[None, :])
    short = 2 * np.pi * (col[:64, None] * grid(256)[None, :]) / NT
    omega_lanes = np.tile(2 * np.pi * (16 * grid(256)[:, None] + grid(16)[None, :]) / NT, (1, 8))
    t = {}
    t["ahead"] = np.concatenate(
        [np.concatenate(split_table(x), 0) for x in (wide, small)], 1
    )
    t["back"] = np.concatenate(split_table(tall) + split_table(small.T), 0)
    twist = np.concatenate([np.cos(short), np.sin(short)], 0)
    omega_part = np.concatenate([np.cos(omega_lanes), -np.sin(omega_lanes)], 0)
    twist = [twist[:, :128], twist[:, 128:]]
    t["shift"] = np.concatenate([omega_part / NT] + twist, 0).astype(np.float32)
    return t


STEP = 2 * math.pi / NT
STEP_HIGH = round(STEP * 2**22) / 2**22
STEP_LOW = STEP - STEP_HIGH
TURN = (6.28125, 2 * math.pi - 6.28125)
TABLES = build_tables()


def iota(shape, dim):
    return lax.broadcasted_iota(jnp.int32, shape, dim)


def halves(value):
    high = value.astype(BF16)
    return high, (value - high.astype(F32)).astype(BF16)


def thirds(value):
    high = value.astype(BF16)
    rest = value - high.astype(F32)
    middle = rest.astype(BF16)
    return high, middle, (rest - middle.astype(F32)).astype(BF16)


def dot(left, right):
    return lax.dot_general(left, right, (((1,), (0,)), ((), ())), preferred_element_type=F32)


def dot_nt(left, right):
    return lax.dot_general(left, right, (((1,), (1,)), ((), ())), preferred_element_type=F32)


def quadrants(product, rows, cols):
    return product[:rows, :cols] + (product[:rows, cols:] + product[rows:, :cols])


def table_times(table, value):
    product = dot(table, jnp.concatenate(halves(value), 1))
    return quadrants(product, table.shape[0] // 2, value.shape[1])


def times_table(value, table):
    product = dot(jnp.concatenate(halves(value), 0), table)
    return quadrants(product, value.shape[0], table.shape[1] // 2)


def sine_cosine_half(angle):
    x = angle * 0.5
    z = x * x
    s = jnp.full_like(z, 1.0 / 6227020800.0)
    for k in (-1.0 / 39916800.0, 1.0 / 362880.0, -1.0 / 5040.0, 1.0 / 120.0, -1.0 / 6.0):
        s = s * z + k
    c = jnp.full_like(z, -1.0 / 87178291200.0)
    for k in (1.0 / 479001600.0, -1.0 / 3628800.0, 1.0 / 40320.0, -1.0 / 720.0, 1.0 / 24.0, -0.5):
        c = c * z + k
    return x + x * (z * s), 1.0 + z * c


def resonance(detune, keep, lost, index):
    index = jnp.where(index > NT // 2, index - NT, index).astype(F32)
    s, c = sine_cosine_half((detune + index * STEP_HIGH) + index * STEP_LOW)
    re = lost + (2.0 * keep) * (s * s)
    im = (2.0 * keep) * (s * c)
    scale = 1.0 / (re * re + im * im)
    return re * scale, -(im * scale)


def cosine_sine(angle):
    s, c = sine_cosine_half(angle)
    return 1.0 - 2.0 * (s * s), 2.0 * (s * c)


def lost_by(rate):
    total = jnp.full_like(rate, 1.0 / 5040.0)
    for k in (-1.0 / 720.0, 1.0 / 120.0, -1.0 / 24.0, 1.0 / 6.0, -0.5, 1.0):
        total = k + rate * total
    return rate * total


def exact_dot(left, right):
    parts = thirds(left)
    return (dot(parts[0], right) + dot(parts[1], right)) + dot(parts[2], right)


def pick_dot(left, right):
    parts = thirds(right)
    return (dot(left, parts[0]) + dot(left, parts[1])) + dot(left, parts[2])


def pick_dot_nt(left, right):
    parts = thirds(right)
    return (dot_nt(left, parts[0]) + dot_nt(left, parts[1])) + dot_nt(left, parts[2])


def bin_columns(decay, detune):
    lost = lost_by(decay)
    keep = 1.0 - lost
    drive = jnp.sqrt(lost_by(2.0 * decay))
    cos, sin = cosine_sine(detune)
    p_re, p_im = keep * cos, -keep * sin
    whole = jnp.exp(-float(NT) * decay)
    far = float(NT) * detune
    turns = jnp.floor(far * (0.5 / math.pi) + 0.5)
    cos, sin = cosine_sine((far - turns * TURN[0]) - turns * TURN[1])
    r_re, r_im = 1.0 - whole * cos, whole * sin
    k_re, k_im = p_re * r_re - p_im * r_im, p_re * r_im + p_im * r_re
    rows = jnp.concatenate(
        [detune, keep, lost, drive, WEIGHT * k_im, -WEIGHT * k_re, keep, keep], 0
    )
    eye = (iota((BINS, BINS), 0) == iota((BINS, BINS), 1)).astype(BF16)
    return pick_dot_nt(eye, rows)


def pack(decay, detune, group_bin, spectral, lateral, occupation):
    parts = [decay, detune, group_bin, spectral, lateral, occupation.T.reshape(-1)]
    starts = [0, BINS, 128, 256, 256 + NT, 256 + NT + NX]
    total = starts[-1] + parts[-1].size
    padded = [
        jnp.pad(part, (start, total - start - part.size)).astype(F32) for part, start in zip(parts, starts)
    ]
    return sum(padded[1:], padded[0]).reshape(total // 128, 128)


def unpack(packed):
    return (packed[0:1, :BINS], packed[0:1, BINS : 2 * BINS], packed[1:2], packed[2:34],
            packed[34:42], packed[42:])


def couplings(drive, group_bin, occupation):
    member = (iota((BINS, GROUPS), 0).astype(F32) == group_bin).astype(BF16)
    return pick_dot_nt(member, occupation) * drive


def prepare_first(packed, quad):
    decay, detune_row, group_bin, spectral, _, occupation = unpack(packed)
    params = bin_columns(decay, detune_row)
    detune, keep, lost, drive = (params[:, k : k + 1] for k in range(4))
    real, imag = [], []
    for w1 in range(16):
        g_re, g_im = resonance(detune, keep, lost, 16 * iota((BINS, 256), 1) + w1)
        real.append(g_re)
        imag.append(g_im)
    resonances = jnp.concatenate(halves(jnp.concatenate(real + imag, 0)), 0)
    per_bin = couplings(drive, group_bin, occupation)
    points = occupation.shape[0]
    pick = iota((points, 128), 0) == 4 * quad + iota((points, 128), 1) // 16 % 4
    chosen = exact_dot(per_bin, pick.astype(BF16))
    lane = iota((BINS, 128), 1)
    couple_row = jnp.sum(
        jnp.where(iota((BINS, 128), 0) == lane // 64 * 16 + lane % 16, chosen, 0.0),
        axis=0, keepdims=True,
    )
    cos, sin = cosine_sine(spectral)
    spectral_parts = cos, sin
    row_of = (iota((256, 32), 0) // 8 == iota((256, 32), 1)).astype(BF16)
    mine = iota((256, 128), 1) // 16 == iota((256, 128), 0) % 8
    lane_of = (iota((128, 128), 0) % 16 == iota((128, 128), 1) % 16).astype(BF16)
    cos = exact_dot(jnp.where(mine, pick_dot(row_of, cos), 0.0), lane_of)
    sin = exact_dot(jnp.where(mine, pick_dot(row_of, sin), 0.0), lane_of)
    index = 16 * iota((256, 128), 0) + iota((256, 128), 1) % 16
    back_re, back_im = cosine_sine(jnp.where(index > NT // 2, NT - index, -index) * STEP)
    wrap_a = (cos * back_re - sin * back_im) * (1.0 / NT)
    wrap_b = (cos * back_im + sin * back_re) * (1.0 / NT)
    index = (iota((64, 256), 0) % 16) * iota((64, 256), 1)
    tc, ts = cosine_sine(jnp.where(index > NT // 2, index - NT, index).astype(F32) * STEP)
    first = jnp.concatenate(
        [tc[:, :128], ts[:, :128], tc[:, 128:], ts[:, 128:],
         jnp.where(iota((256, 128), 1) < 64, wrap_a, wrap_b),
         jnp.broadcast_to(couple_row, (8, 128))],
        0,
    )
    return resonances, first, params, per_bin, spectral_parts


def prepare_rest(packed, made, here, quad):
    lateral = unpack(packed)[4]
    resonances, _, params, per_bin, (cos, sin) = made
    points = per_bin.shape[1]
    pick_rows = iota((64, points), 1) == 4 * quad + iota((64, points), 0) // 16
    spread = pick_dot_nt(pick_rows.astype(BF16), jnp.concatenate([per_bin] * 16, 0))
    couple_grid = jnp.where(
        iota((64, 512), 1) // 32 == iota((64, 512), 0) % 16, spread, 0.0
    )
    gain_high, gain_low = halves(couple_grid * WEIGHT)
    gain = dot(jnp.concatenate([gain_high, gain_low], 0),
               jnp.concatenate([resonances[:512], resonances[512:1024]], 1))
    gain_rest = dot(gain_high, jnp.concatenate([resonances[1024:1536], resonances[1536:]], 1))
    gain = (gain[:64] + gain[64:]) + gain_rest
    gain = jnp.concatenate([-gain[:, 256:], gain[:, :256]], 0)
    own = (iota((32, 128), 0) == here // 8) & (iota((32, 128), 1) // 16 == here % 8)
    lane_of = (iota((128, 128), 0) % 16 == iota((128, 128), 1) % 16).astype(BF16)
    own_rows = [jnp.sum(jnp.where(own, x, 0.0), axis=0, keepdims=True) for x in (cos, sin)]
    own_rows = exact_dot(jnp.concatenate(own_rows * 4, 0), lane_of)
    once_re, once_im = own_rows[0:1], own_rows[1:2]
    eye = (iota((128, 128), 0) == iota((128, 128), 1)).astype(BF16)
    cos, sin = cosine_sine(lateral)
    cos, sin = pick_dot_nt(eye, cos), pick_dot_nt(eye, sin)
    r, i = (
        [
            jnp.concatenate([x[:, 2 * k : 2 * k + 1], x[:, 2 * k + 1 : 2 * k + 2]], 0)
            for k in range(4)
        ]
        for x in (cos, sin)
    )
    blocks_re = [
        (r[0] + r[2]) + (r[1] + r[3]),
        (r[0] - r[2]) + (i[1] - i[3]),
        (r[0] + r[2]) - (r[1] + r[3]),
        (r[0] - r[2]) - (i[1] - i[3]),
    ]
    blocks_im = [
        (i[0] + i[2]) + (i[1] + i[3]),
        (i[0] - i[2]) - (r[1] - r[3]),
        (i[0] + i[2]) - (i[1] + i[3]),
        (i[0] - i[2]) + (r[1] - r[3]),
    ]
    eight = iota((256, 128), 1) // 16
    index = iota((256, 128), 0)
    cos1, sin1 = cosine_sine(index.astype(F32) * (-2.0 * math.pi / NX))
    cos2, sin2 = cos1 * cos1 - sin1 * sin1, 2.0 * (cos1 * sin1)
    cos3, sin3 = cos1 * cos2 - sin1 * sin2, cos1 * sin2 + sin1 * cos2
    turns = [None, (cos1, sin1), (cos2, sin2), (cos3, sin3)]
    mixing = []
    for k in range(4):
        re, im = blocks_re[k] * (1.0 / NX), blocks_im[k] * (1.0 / NX)
        if k == 0:
            real, imag = re, im
        else:
            near = eight % 4 + k < 4
            cos = jnp.where(near, turns[k][0], turns[4 - k][0])
            sin = jnp.where(near, turns[k][1], -turns[4 - k][1])
            real, imag = cos * re - sin * im, cos * im + sin * re
        mixing.append(jnp.where(eight < 4, real, imag))
    mixing = jnp.concatenate(mixing, 0)
    rows = jnp.concatenate([params[:16]] * 4 + [params[16:]] * 4, 0)
    g_re, g_im = resonance(
        rows[:, 0:1], rows[:, 1:2], rows[:, 2:3], 16 * here + iota((128, 128), 1) % 16
    )
    twice_re = once_re * once_re - once_im * once_im
    twice_im = 2.0 * once_re * once_im
    inside = iota((128, 128), 0) // 16 % 4 == iota((128, 128), 1) // 16 % 4
    left = iota((128, 128), 1) < 64
    f_re, f_im = -WEIGHT * twice_im, WEIGHT * twice_re
    b_re = jnp.where(inside, g_re * f_re - g_im * f_im, 0.0)
    b_im = jnp.where(inside, g_re * f_im + g_im * f_re, 0.0)
    gain_here = jnp.concatenate([b_re, jnp.where(left, -b_im, b_im)], 1)
    gain_here = jnp.concatenate(halves(gain_here), 0)
    side_row = jnp.where(iota((1, 128), 1) < 64, -1.0, 1.0)
    twice = jnp.concatenate([twice_re] * 8 + [twice_im * side_row] * 8, 0)
    k_re, k_im = rows[:, 4:5], rows[:, 5:6]
    f_re = once_re * k_re - once_im * k_im
    f_im = once_re * k_im + once_im * k_re
    h_re = jnp.where(inside, g_re * f_re - g_im * f_im, 0.0)
    h_im = jnp.where(inside, g_re * f_im + g_im * f_re, 0.0)
    top, bottom = jnp.where(left, h_re, h_im), jnp.where(left, -h_im, h_re)
    wrap_here = jnp.concatenate([top[:64], bottom[:64], top[64:], bottom[64:]], 0)
    wrap_here = jnp.concatenate(halves(wrap_here), 1)
    second = jnp.concatenate([twice, mixing], 0)
    second_tables = jnp.concatenate([gain_here, wrap_here], 0)
    turned = [jnp.broadcast_to(params[:, k : k + 1], (BINS, 128)) for k in (4, 5)]
    third = jnp.concatenate(
        [couple_grid[:, 128 * k : 128 * k + 128] for k in range(4)]
        + [gain[:, :128], gain[:, 128:]] + turned, 0,
    )
    return second, second_tables, third


def half_sign(shape):
    return jnp.where(iota(shape, 1) < 64, -1.0, 1.0)


def wrap_state(resonances, weighted, roll):
    product = dot(resonances, jnp.concatenate(halves(weighted), 1))
    product = quadrants(product, 1024, 128)
    lane = iota((BINS, 128), 1) % 16
    sums = []
    for part in range(2):
        total = jnp.zeros((BINS, 128), F32)
        for w1 in range(16):
            start = (part * 16 + w1) * BINS
            total = total + jnp.where(lane == w1, product[start : start + BINS], 0.0)
        sums.append(total)
    return sums[0] + half_sign((BINS, 128)) * roll(sums[1], 64)


def unfold(pair, roll):
    turned = roll(pair, 64)
    left = iota((256, 128), 1) < 64
    return jnp.where(left, pair, turned), jnp.where(left, -turned, pair)


def untwist(pair):
    return (jnp.concatenate([pair[k : k + 64], pair[128 + k : 192 + k]], 1) for k in (0, 64))


def to_rows(field, first, resonances, ahead, roll):
    mixed = table_times(ahead[:, 512:], field)
    mixed = jnp.concatenate([mixed[:128], mixed[128:]], 1)
    re, im = mixed[:64], mixed[64:]
    tc, ts = untwist(first)
    re, im = re * tc + im * ts, im * tc - re * ts
    both = jnp.concatenate(
        [jnp.concatenate([re, im], 1), jnp.concatenate([im, -re], 1)], 0
    )
    product = dot_nt(ahead[:, :512], jnp.concatenate(halves(both), 0))
    spectrum = quadrants(product, 256, 128)
    wrap_a, wrap_b = unfold(first[256:512], roll)
    weighted = wrap_a * spectrum + wrap_b * roll(spectrum, 64)
    state = wrap_state(resonances[...], weighted, roll)
    place = (iota((128, 256), 0) // 16 == iota((128, 256), 1) % 128 // 16).astype(BF16)
    parts = exact_dot(state, place)
    lane = iota((BINS, 256), 1)
    chosen = iota((BINS, 256), 0) == lane // 128 * 16 + lane % 16
    state_row = jnp.sum(jnp.where(chosen, parts, 0.0), axis=0, keepdims=True)
    return spectrum, state_row[:, :128], state_row[:, 128:], first[512:513]


def diffract(blocks, wide, mixing, roll):
    sign = half_sign((256, 128))

    def transform(parts, direction):
        columns = []
        for part in parts:
            turned = roll(part, 64) * (sign * (-direction))
            columns += list(halves(jnp.concatenate([part, turned], 0)))
        product = dot(wide, jnp.concatenate(columns, 1))
        return [
            quadrants(product[:, 256 * k : 256 * k + 256], 256, 128) for k in range(len(parts))
        ]

    spectra = transform(blocks, 1.0)
    mixed = []
    for part in spectra:
        total = mixing[0] * part
        for r in range(1, 8):
            total = total + mixing[r] * roll(part, 128 - 16 * r)
        mixed.append(total)
    return transform(mixed, -1.0)


def columns_step(message, wide, second, second_tables, roll):
    field, state0, state1, couple = message
    eight = iota((256, 128), 1) // 16
    mixing = [None] * 8
    for k in range(4):
        real, imag = unfold(second[16 + 256 * k : 272 + 256 * k], roll)
        for r in (k, k + 4):
            mixing[r] = jnp.where((eight + r) % 8 // 4 == eight // 4, real, imag)
    field, state0, state1 = diffract([field, state0, state1], wide, mixing, roll)
    product = dot(jnp.concatenate(halves(couple), 0), second_tables[:128])
    rest = dot(couple.astype(BF16), second_tables[128:256])
    factor = (product[:256] + product[256:]) + rest
    turned = roll(couple, 64)
    left = iota((256, 128), 1) < 64
    states = jnp.concatenate(
        [state0 * jnp.where(left, couple, turned), state1 * jnp.where(left, turned, couple)], 1
    )
    wrapped = times_table(states, second_tables[256:])
    straight, crossed = factor[:, :128] + second[0:1], factor[:, 128:] + second[8:9]
    field = straight * field + crossed * roll(field, 64) + wrapped
    return diffract([field], wide, mixing, roll)[0]


def to_blocks(spectrum, resonances, third, back, shift, roll):
    sign = half_sign((256, 128))
    weighted = shift[:256] * spectrum + (shift[256:512] * sign) * roll(spectrum, 64)
    state = wrap_state(resonances[...], weighted, roll)
    state = third[512:544] * state + third[544:576] * (
        half_sign((BINS, 128)) * roll(state, 64)
    )
    gather = (iota((128, 128), 0) // 16 == iota((128, 128), 1) // 16).astype(BF16)
    spread = sum(dot_nt(gather, jnp.concatenate([part] * 16, 0)) for part in thirds(state))
    couple_grid = jnp.concatenate([third[64 * k : 64 * k + 64] for k in range(4)], 1)
    k_re, k_im = couple_grid * spread[:64], couple_grid * spread[64:]
    left = jnp.concatenate(
        [jnp.concatenate([k_re, -k_im], 1), jnp.concatenate([k_im, k_re], 1)], 0
    )
    left_high, left_low = halves(left)
    wrapped = dot(jnp.concatenate([left_high, left_low], 0), resonances[:1024])
    wrapped = (wrapped[:128] + wrapped[128:]) + dot(left_high, resonances[1024:])
    turned = spectrum.T
    re, im = turned[:64], turned[64:]
    gain = jnp.concatenate([third[256:384], third[384:512]], 1)
    gain_re, gain_im = gain[:64], gain[64:]
    out_re = re + (re * gain_re - im * gain_im) + wrapped[:64]
    out_im = im + (re * gain_im + im * gain_re) + wrapped[64:]
    both = jnp.concatenate(
        [jnp.concatenate([out_re, -out_im], 1), jnp.concatenate([out_im, out_re], 1)], 0
    )
    high, low = halves(both)
    mixed = dot(jnp.concatenate([high, low], 0), back[:512])
    mixed = (mixed[:128] + mixed[128:]) + dot(high, back[512:1024])
    re, im = mixed[:64], mixed[64:]
    tc, ts = untwist(shift[512:])
    re, im = re * tc - im * ts, im * tc + re * ts
    mixed = jnp.concatenate(
        [re[:, :128], im[:, :128], re[:, 128:], im[:, 128:]], 0
    ) * (1.0 / NT)
    return table_times(back[1024:], mixed)


def lane_roll(value, shift):
    return pltpu.roll(value, shift, 1)


def shape(*dims, dtype=F32):
    return jax.ShapeDtypeStruct(dims, dtype)


VMEM_SPEC = pl.BlockSpec(memory_space=pltpu.VMEM)
HBM_SPEC = pl.BlockSpec(memory_space=pltpu.HBM)


def call(kernel, out_shape, in_specs, out_specs, scratch, *operands, flops, limit=40):
    moved = sum(x.size * x.dtype.itemsize for x in operands)
    return pl.pallas_call(
        kernel,
        out_shape=out_shape,
        in_specs=in_specs,
        out_specs=out_specs,
        scratch_shapes=scratch,
        compiler_params=pltpu.CompilerParams(vmem_limit_bytes=limit * 1024 * 1024),
        cost_estimate=pl.CostEstimate(flops=flops, bytes_accessed=moved, transcendentals=0),
    )(*operands)


def halves_of_tiles(upper, lower):
    low = iota((8, 128), 0) < 4
    return (
        jnp.where(low, upper, pltpu.roll(lower, 4, 0)),
        jnp.where(low, pltpu.roll(upper, 4, 0), lower),
    )


def cut_kernel(field, out):
    for c in range(2):
        for row in range(8):
            tile = field[c, 8 * row : 8 * row + 8, :]
            first, second = halves_of_tiles(tile[:, :128], tile[:, 128:])
            out[32 * row + 8 * c : 32 * row + 8 * c + 8, :] = first
            out[32 * row + 16 + 8 * c : 32 * row + 24 + 8 * c, :] = second


def join_kernel(rows, field, buffer, sems):
    copies = []
    for c in range(2):
        for row in range(8):
            first = rows[32 * row + 8 * c : 32 * row + 8 * c + 8, :]
            second = rows[32 * row + 16 + 8 * c : 32 * row + 24 + 8 * c, :]
            upper, lower = halves_of_tiles(first, second)
            buffer[c, 8 * row : 8 * row + 8, :128] = upper
            buffer[c, 8 * row : 8 * row + 8, 128:] = lower
        copies.append(pltpu.make_async_copy(buffer.at[c], field.at[c], sems.at[c]))
        copies[-1].start()
    for copy in copies:
        copy.wait()


PREPARED = (shape(2560, 256, dtype=BF16), shape(2136, 128))


def prepare_kernel(packed, tables, later):
    quad = lax.axis_index("tm")
    here = lax.axis_index("lat") * 16 + quad
    packed = packed[...]
    made = prepare_first(packed, quad)
    second, second_tables, third = prepare_rest(packed, made, here, quad)
    tables[:2048] = made[0]
    tables[2048:] = second_tables
    later[:1040] = second
    later[1040:1616] = third
    later[1616:] = made[1]


def rows_kernel(field, tables, later, ahead, out):
    spectrum, *rest = to_rows(
        field[...], later[1616:], tables.at[:2048], ahead, lane_roll
    )
    out[pl.ds(0, 256, stride=4), :] = spectrum
    for k, row in enumerate(rest):
        out[pl.ds(k + 1, 256, stride=4), :] = jnp.broadcast_to(row, (256, 128))


def columns_kernel(message, ahead, tables, later, out):
    parts = [message[pl.ds(k, 256, stride=4), :] for k in range(4)]
    out[...] = columns_step(parts, ahead[:, :512], later, tables[2048:], lane_roll)


def blocks_kernel(spectrum, tables, later, back, shift, out):
    out[...] = to_blocks(
        spectrum[...], tables[:2048], later[1040:1616], back[...], shift[...], lane_roll
    )


def on_device(
    light_field, lateral_phase, spectral_phase, occupation, bin_decay, bin_detune, group_bin
):
    t = {name: jnp.asarray(value) for name, value in TABLES.items()}
    sems = pltpu.SemaphoreType.DMA
    rows = call(
        cut_kernel, shape(256, 128), [VMEM_SPEC], VMEM_SPEC, [], light_field, flops=1000
    )
    rows = lax.all_to_all(rows.reshape(16, 16, 128), "tm", 0, 0, tiled=True)
    packed = pack(
        bin_decay, bin_detune, group_bin, spectral_phase, lateral_phase, occupation
    )
    tables, later = call(
        prepare_kernel, PREPARED, [VMEM_SPEC], (VMEM_SPEC,) * 2, [], packed, flops=4_000_000_000
    )
    message = call(
        rows_kernel, shape(1024, 128), [VMEM_SPEC] * 4, VMEM_SPEC, [],
        rows.reshape(256, 128), tables, later, t["ahead"],
        flops=1_500_000_000,
    )
    message = lax.all_to_all(message.reshape(256, 4, 128), BOTH, 0, 0, tiled=True)
    columns = call(
        columns_kernel, shape(256, 128), [VMEM_SPEC] * 4, VMEM_SPEC, [],
        message.reshape(1024, 128), t["ahead"], tables, later, flops=3_000_000_000,
    )
    spectrum = lax.all_to_all(columns, BOTH, 0, 0, tiled=True)
    finished = call(
        blocks_kernel, shape(256, 128), [VMEM_SPEC] * 5, VMEM_SPEC, [],
        spectrum, tables, later, t["back"], t["shift"], flops=2_300_000_000,
    )
    turned = lax.all_to_all(finished.reshape(16, 16, 128), "tm", 0, 0, tiled=True)
    return call(
        join_kernel, shape(2, 64, 256), [VMEM_SPEC], HBM_SPEC,
        [pltpu.VMEM((2, 64, 256), F32), sems((2,))], turned.reshape(256, 128), flops=1000,
    )


def solution(mesh):
    return jax.shard_map(
        on_device,
        mesh=mesh,
        in_specs=(P(None, "lat", "tm"), P(), P(), P(None, "lat"), P(), P(), P()),
        out_specs=P(None, "lat", "tm"),
        check_vma=False,
    )
```

```python
import math

import jax
import jax.numpy as jnp
import numpy as np
from jax import lax
from jax.experimental import pallas as pl
from jax.experimental.pallas import tpu as pltpu
from jax.sharding import PartitionSpec as P

NX, NT, BINS, GROUPS = 1024, 4096, 32, 128
WEIGHT = 0.5 / math.sqrt(GROUPS)
F32, BF16 = jnp.float32, jnp.bfloat16
BOTH = ("lat", "tm")


def split_table(table):
    high = table.astype(np.float32).astype(jnp.bfloat16)
    low = (table - high.astype(np.float64)).astype(jnp.bfloat16)
    return high, low


def build_tables():
    grid = np.arange
    angle = 2 * np.pi * (grid(256)[:, None] * grid(256)[None, :] % 256) / 256
    wide = np.concatenate([np.cos(angle), np.sin(angle)], 1)
    tall = np.concatenate([np.cos(angle), np.sin(angle)], 0)
    lane = grid(128)
    c, q, col = lane // 64, lane // 16 % 4, lane % 16
    to, row = grid(256), grid(256)
    th, tc, tq, tw = to // 128, to // 64 % 2, to // 16 % 4, to % 16
    rm, rc, rh, rq = row // 16, row // 8 % 2, row // 4 % 2, row % 4
    turn = 2 * np.pi * (tw[:, None] * rm[None, :] % 16) / 16
    sign = np.where(tc[:, None] == 0, 1.0, -1.0)
    small = np.where(tc[:, None] == rc[None, :], np.cos(turn), sign * np.sin(turn))
    small = small * (tq[:, None] == rq[None, :]) * (th[:, None] == rh[None, :])
    short = 2 * np.pi * (col[:64, None] * grid(256)[None, :]) / NT
    omega_lanes = np.tile(2 * np.pi * (16 * grid(256)[:, None] + grid(16)[None, :]) / NT, (1, 8))
    t = {}
    t["ahead"] = np.concatenate(
        [np.concatenate(split_table(x), 0) for x in (wide, small)], 1
    )
    t["back"] = np.concatenate(split_table(tall) + split_table(small.T), 0)
    twist = np.concatenate([np.cos(short), np.sin(short)], 0)
    omega_part = np.concatenate([np.cos(omega_lanes), -np.sin(omega_lanes)], 0)
    twist = [twist[:, :128], twist[:, 128:]]
    t["shift"] = np.concatenate([omega_part / NT] + twist, 0).astype(np.float32)
    return t


STEP = 2 * math.pi / NT
STEP_HIGH = round(STEP * 2**22) / 2**22
STEP_LOW = STEP - STEP_HIGH
TURN = (6.28125, 2 * math.pi - 6.28125)
TABLES = build_tables()


def iota(shape, dim):
    return lax.broadcasted_iota(jnp.int32, shape, dim)


def halves(value):
    high = value.astype(BF16)
    return high, (value - high.astype(F32)).astype(BF16)


def thirds(value):
    high = value.astype(BF16)
    rest = value - high.astype(F32)
    middle = rest.astype(BF16)
    return high, middle, (rest - middle.astype(F32)).astype(BF16)


def dot(left, right):
    return lax.dot_general(left, right, (((1,), (0,)), ((), ())), preferred_element_type=F32)


def dot_nt(left, right):
    return lax.dot_general(left, right, (((1,), (1,)), ((), ())), preferred_element_type=F32)


def quadrants(product, rows, cols):
    rest = product[:rows, cols:] + (product[rows:, :cols] + product[rows:, cols:])
    return product[:rows, :cols] + rest


def table_times(table, value):
    product = dot(table, jnp.concatenate(halves(value), 1))
    return quadrants(product, table.shape[0] // 2, value.shape[1])


def times_table(value, table):
    product = dot(jnp.concatenate(halves(value), 0), table)
    return quadrants(product, value.shape[0], table.shape[1] // 2)


def sine_cosine_half(angle):
    x = angle * 0.5
    z = x * x
    s = jnp.full_like(z, 1.0 / 6227020800.0)
    for k in (-1.0 / 39916800.0, 1.0 / 362880.0, -1.0 / 5040.0, 1.0 / 120.0, -1.0 / 6.0):
        s = s * z + k
    c = jnp.full_like(z, -1.0 / 87178291200.0)
    for k in (1.0 / 479001600.0, -1.0 / 3628800.0, 1.0 / 40320.0, -1.0 / 720.0, 1.0 / 24.0, -0.5):
        c = c * z + k
    return x + x * (z * s), 1.0 + z * c


def resonance(detune, keep, lost, index):
    index = jnp.where(index > NT // 2, index - NT, index).astype(F32)
    s, c = sine_cosine_half((detune + index * STEP_HIGH) + index * STEP_LOW)
    re = lost + (2.0 * keep) * (s * s)
    im = (2.0 * keep) * (s * c)
    scale = 1.0 / (re * re + im * im)
    return re * scale, -(im * scale)


def cosine_sine(angle):
    s, c = sine_cosine_half(angle)
    return 1.0 - 2.0 * (s * s), 2.0 * (s * c)


def lost_by(rate):
    total = jnp.full_like(rate, 1.0 / 5040.0)
    for k in (-1.0 / 720.0, 1.0 / 120.0, -1.0 / 24.0, 1.0 / 6.0, -0.5, 1.0):
        total = k + rate * total
    return rate * total


def exact_dot(left, right):
    parts = thirds(left)
    return (dot(parts[0], right) + dot(parts[1], right)) + dot(parts[2], right)


def pick_dot(left, right):
    parts = thirds(right)
    return (dot(left, parts[0]) + dot(left, parts[1])) + dot(left, parts[2])


def pick_dot_nt(left, right):
    parts = thirds(right)
    return (dot_nt(left, parts[0]) + dot_nt(left, parts[1])) + dot_nt(left, parts[2])


def bin_columns(decay, detune):
    lost = lost_by(decay)
    keep = 1.0 - lost
    drive = jnp.sqrt(lost_by(2.0 * decay))
    cos, sin = cosine_sine(detune)
    p_re, p_im = keep * cos, -keep * sin
    whole = jnp.exp(-float(NT) * decay)
    far = float(NT) * detune
    turns = jnp.floor(far * (0.5 / math.pi) + 0.5)
    cos, sin = cosine_sine((far - turns * TURN[0]) - turns * TURN[1])
    r_re, r_im = 1.0 - whole * cos, whole * sin
    k_re, k_im = p_re * r_re - p_im * r_im, p_re * r_im + p_im * r_re
    rows = jnp.concatenate(
        [detune, keep, lost, drive, WEIGHT * k_im, -WEIGHT * k_re, keep, keep], 0
    )
    eye = (iota((BINS, BINS), 0) == iota((BINS, BINS), 1)).astype(BF16)
    return pick_dot_nt(eye, rows)


def pack(decay, detune, group_bin, spectral, lateral, occupation):
    parts = [decay, detune, group_bin, spectral, lateral, occupation.T.reshape(-1)]
    starts = [0, BINS, 128, 256, 256 + NT, 256 + NT + NX]
    total = starts[-1] + parts[-1].size
    padded = [
        jnp.pad(part, (start, total - start - part.size)).astype(F32) for part, start in zip(parts, starts)
    ]
    return sum(padded[1:], padded[0]).reshape(total // 128, 128)


def unpack(packed):
    return (packed[0:1, :BINS], packed[0:1, BINS : 2 * BINS], packed[1:2], packed[2:34],
            packed[34:42], packed[42:])


def couplings(drive, group_bin, occupation):
    member = (iota((BINS, GROUPS), 0).astype(F32) == group_bin).astype(BF16)
    return pick_dot_nt(member, occupation) * drive


def prepare_first(packed, quad):
    decay, detune_row, group_bin, spectral, _, occupation = unpack(packed)
    params = bin_columns(decay, detune_row)
    detune, keep, lost, drive = (params[:, k : k + 1] for k in range(4))
    real, imag = [], []
    for w1 in range(16):
        g_re, g_im = resonance(detune, keep, lost, 16 * iota((BINS, 256), 1) + w1)
        real.append(g_re)
        imag.append(g_im)
    resonances = jnp.concatenate(halves(jnp.concatenate(real + imag, 0)), 0)
    per_bin = couplings(drive, group_bin, occupation)
    points = occupation.shape[0]
    pick = iota((points, 128), 0) == 4 * quad + iota((points, 128), 1) // 16 % 4
    chosen = exact_dot(per_bin, pick.astype(BF16))
    lane = iota((BINS, 128), 1)
    couple_row = jnp.sum(
        jnp.where(iota((BINS, 128), 0) == lane // 64 * 16 + lane % 16, chosen, 0.0),
        axis=0, keepdims=True,
    )
    cos, sin = cosine_sine(spectral)
    spectral_parts = cos, sin
    row_of = (iota((256, 32), 0) // 8 == iota((256, 32), 1)).astype(BF16)
    mine = iota((256, 128), 1) // 16 == iota((256, 128), 0) % 8
    lane_of = (iota((128, 128), 0) % 16 == iota((128, 128), 1) % 16).astype(BF16)
    cos = exact_dot(jnp.where(mine, pick_dot(row_of, cos), 0.0), lane_of)
    sin = exact_dot(jnp.where(mine, pick_dot(row_of, sin), 0.0), lane_of)
    index = 16 * iota((256, 128), 0) + iota((256, 128), 1) % 16
    back_re, back_im = cosine_sine(jnp.where(index > NT // 2, NT - index, -index) * STEP)
    wrap_a = (cos * back_re - sin * back_im) * (1.0 / NT)
    wrap_b = (cos * back_im + sin * back_re) * (1.0 / NT)
    index = (iota((64, 256), 0) % 16) * iota((64, 256), 1)
    tc, ts = cosine_sine(jnp.where(index > NT // 2, index - NT, index).astype(F32) * STEP)
    first = jnp.concatenate(
        [tc[:, :128], ts[:, :128], tc[:, 128:], ts[:, 128:],
         jnp.where(iota((256, 128), 1) < 64, wrap_a, wrap_b),
         jnp.broadcast_to(couple_row, (8, 128))],
        0,
    )
    return resonances, first, params, per_bin, spectral_parts


def prepare_rest(packed, made, here, quad):
    lateral = unpack(packed)[4]
    resonances, _, params, per_bin, (cos, sin) = made
    points = per_bin.shape[1]
    pick_rows = iota((64, points), 1) == 4 * quad + iota((64, points), 0) // 16
    spread = pick_dot_nt(pick_rows.astype(BF16), jnp.concatenate([per_bin] * 16, 0))
    couple_grid = jnp.where(
        iota((64, 512), 1) // 32 == iota((64, 512), 0) % 16, spread, 0.0
    )
    gain_high, gain_low = halves(couple_grid * WEIGHT)
    gain = dot(jnp.concatenate([gain_high, gain_low], 0),
               jnp.concatenate([resonances[:512], resonances[512:1024]], 1))
    gain_rest = dot(gain_high, jnp.concatenate([resonances[1024:1536], resonances[1536:]], 1))
    gain = (gain[:64] + gain[64:]) + gain_rest
    gain = jnp.concatenate([-gain[:, 256:], gain[:, :256]], 0)
    own = (iota((32, 128), 0) == here // 8) & (iota((32, 128), 1) // 16 == here % 8)
    lane_of = (iota((128, 128), 0) % 16 == iota((128, 128), 1) % 16).astype(BF16)
    own_rows = [jnp.sum(jnp.where(own, x, 0.0), axis=0, keepdims=True) for x in (cos, sin)]
    own_rows = exact_dot(jnp.concatenate(own_rows * 4, 0), lane_of)
    once_re, once_im = own_rows[0:1], own_rows[1:2]
    eye = (iota((128, 128), 0) == iota((128, 128), 1)).astype(BF16)
    cos, sin = cosine_sine(lateral)
    cos, sin = pick_dot_nt(eye, cos), pick_dot_nt(eye, sin)
    r, i = (
        [
            jnp.concatenate([x[:, 2 * k : 2 * k + 1], x[:, 2 * k + 1 : 2 * k + 2]], 0)
            for k in range(4)
        ]
        for x in (cos, sin)
    )
    blocks_re = [
        (r[0] + r[2]) + (r[1] + r[3]),
        (r[0] - r[2]) + (i[1] - i[3]),
        (r[0] + r[2]) - (r[1] + r[3]),
        (r[0] - r[2]) - (i[1] - i[3]),
    ]
    blocks_im = [
        (i[0] + i[2]) + (i[1] + i[3]),
        (i[0] - i[2]) - (r[1] - r[3]),
        (i[0] + i[2]) - (i[1] + i[3]),
        (i[0] - i[2]) + (r[1] - r[3]),
    ]
    eight = iota((256, 128), 1) // 16
    index = iota((256, 128), 0)
    cos1, sin1 = cosine_sine(index.astype(F32) * (-2.0 * math.pi / NX))
    cos2, sin2 = cos1 * cos1 - sin1 * sin1, 2.0 * (cos1 * sin1)
    cos3, sin3 = cos1 * cos2 - sin1 * sin2, cos1 * sin2 + sin1 * cos2
    turns = [None, (cos1, sin1), (cos2, sin2), (cos3, sin3)]
    mixing = []
    for k in range(4):
        re, im = blocks_re[k] * (1.0 / NX), blocks_im[k] * (1.0 / NX)
        if k == 0:
            real, imag = re, im
        else:
            near = eight % 4 + k < 4
            cos = jnp.where(near, turns[k][0], turns[4 - k][0])
            sin = jnp.where(near, turns[k][1], -turns[4 - k][1])
            real, imag = cos * re - sin * im, cos * im + sin * re
        mixing.append(jnp.where(eight < 4, real, imag))
    mixing = jnp.concatenate(mixing, 0)
    rows = jnp.concatenate([params[:16]] * 4 + [params[16:]] * 4, 0)
    g_re, g_im = resonance(
        rows[:, 0:1], rows[:, 1:2], rows[:, 2:3], 16 * here + iota((128, 128), 1) % 16
    )
    twice_re = once_re * once_re - once_im * once_im
    twice_im = 2.0 * once_re * once_im
    inside = iota((128, 128), 0) // 16 % 4 == iota((128, 128), 1) // 16 % 4
    left = iota((128, 128), 1) < 64
    f_re, f_im = -WEIGHT * twice_im, WEIGHT * twice_re
    b_re = jnp.where(inside, g_re * f_re - g_im * f_im, 0.0)
    b_im = jnp.where(inside, g_re * f_im + g_im * f_re, 0.0)
    gain_here = jnp.concatenate([b_re, jnp.where(left, -b_im, b_im)], 1)
    gain_here = jnp.concatenate(halves(gain_here), 0)
    side_row = jnp.where(iota((1, 128), 1) < 64, -1.0, 1.0)
    twice = jnp.concatenate([twice_re] * 8 + [twice_im * side_row] * 8, 0)
    k_re, k_im = rows[:, 4:5], rows[:, 5:6]
    f_re = once_re * k_re - once_im * k_im
    f_im = once_re * k_im + once_im * k_re
    h_re = jnp.where(inside, g_re * f_re - g_im * f_im, 0.0)
    h_im = jnp.where(inside, g_re * f_im + g_im * f_re, 0.0)
    top, bottom = jnp.where(left, h_re, h_im), jnp.where(left, -h_im, h_re)
    wrap_here = jnp.concatenate([top[:64], bottom[:64], top[64:], bottom[64:]], 0)
    wrap_here = jnp.concatenate(halves(wrap_here), 1)
    second = jnp.concatenate([twice, mixing], 0)
    second_tables = jnp.concatenate([gain_here, wrap_here], 0)
    turned = [jnp.broadcast_to(params[:, k : k + 1], (BINS, 128)) for k in (4, 5)]
    third = jnp.concatenate(
        [couple_grid[:, 128 * k : 128 * k + 128] for k in range(4)]
        + [gain[:, :128], gain[:, 128:]] + turned, 0,
    )
    return second, second_tables, third


def half_sign(shape):
    return jnp.where(iota(shape, 1) < 64, -1.0, 1.0)


def wrap_state(resonances, weighted, roll):
    product = dot(resonances, jnp.concatenate(halves(weighted), 1))
    product = quadrants(product, 1024, 128)
    lane = iota((BINS, 128), 1) % 16
    sums = []
    for part in range(2):
        total = jnp.zeros((BINS, 128), F32)
        for w1 in range(16):
            start = (part * 16 + w1) * BINS
            total = total + jnp.where(lane == w1, product[start : start + BINS], 0.0)
        sums.append(total)
    return sums[0] + half_sign((BINS, 128)) * roll(sums[1], 64)


def unfold(pair, roll):
    turned = roll(pair, 64)
    left = iota((256, 128), 1) < 64
    return jnp.where(left, pair, turned), jnp.where(left, -turned, pair)


def untwist(pair):
    return (jnp.concatenate([pair[k : k + 64], pair[128 + k : 192 + k]], 1) for k in (0, 64))


def to_rows(field, first, resonances, ahead, roll):
    mixed = table_times(ahead[:, 512:], field)
    mixed = jnp.concatenate([mixed[:128], mixed[128:]], 1)
    re, im = mixed[:64], mixed[64:]
    tc, ts = untwist(first)
    re, im = re * tc + im * ts, im * tc - re * ts
    both = jnp.concatenate(
        [jnp.concatenate([re, im], 1), jnp.concatenate([im, -re], 1)], 0
    )
    product = dot_nt(ahead[:, :512], jnp.concatenate(halves(both), 0))
    spectrum = quadrants(product, 256, 128)
    wrap_a, wrap_b = unfold(first[256:512], roll)
    weighted = wrap_a * spectrum + wrap_b * roll(spectrum, 64)
    state = wrap_state(resonances[...], weighted, roll)
    place = (iota((128, 256), 0) // 16 == iota((128, 256), 1) % 128 // 16).astype(BF16)
    parts = exact_dot(state, place)
    lane = iota((BINS, 256), 1)
    chosen = iota((BINS, 256), 0) == lane // 128 * 16 + lane % 16
    state_row = jnp.sum(jnp.where(chosen, parts, 0.0), axis=0, keepdims=True)
    return spectrum, state_row[:, :128], state_row[:, 128:], first[512:513]


def diffract(blocks, wide, mixing, roll):
    sign = half_sign((256, 128))

    def transform(parts, direction):
        columns = []
        for part in parts:
            turned = roll(part, 64) * (sign * (-direction))
            columns += list(halves(jnp.concatenate([part, turned], 0)))
        product = dot(wide, jnp.concatenate(columns, 1))
        return [
            quadrants(product[:, 256 * k : 256 * k + 256], 256, 128) for k in range(len(parts))
        ]

    spectra = transform(blocks, 1.0)
    mixed = []
    for part in spectra:
        total = mixing[0] * part
        for r in range(1, 8):
            total = total + mixing[r] * roll(part, 128 - 16 * r)
        mixed.append(total)
    return transform(mixed, -1.0)


def columns_step(message, wide, second, second_tables, roll):
    field, state0, state1, couple = message
    eight = iota((256, 128), 1) // 16
    mixing = [None] * 8
    for k in range(4):
        real, imag = unfold(second[16 + 256 * k : 272 + 256 * k], roll)
        for r in (k, k + 4):
            mixing[r] = jnp.where((eight + r) % 8 // 4 == eight // 4, real, imag)
    field, state0, state1 = diffract([field, state0, state1], wide, mixing, roll)
    product = dot(jnp.concatenate(halves(couple), 0), second_tables[:128])
    rest = dot(couple.astype(BF16), second_tables[128:256])
    factor = (product[:256] + product[256:]) + rest
    turned = roll(couple, 64)
    left = iota((256, 128), 1) < 64
    states = jnp.concatenate(
        [state0 * jnp.where(left, couple, turned), state1 * jnp.where(left, turned, couple)], 1
    )
    wrapped = times_table(states, second_tables[256:])
    straight, crossed = factor[:, :128] + second[0:1], factor[:, 128:] + second[8:9]
    field = straight * field + crossed * roll(field, 64) + wrapped
    return diffract([field], wide, mixing, roll)[0]


def to_blocks(spectrum, resonances, third, back, shift, roll):
    sign = half_sign((256, 128))
    weighted = shift[:256] * spectrum + (shift[256:512] * sign) * roll(spectrum, 64)
    state = wrap_state(resonances[...], weighted, roll)
    state = third[512:544] * state + third[544:576] * (
        half_sign((BINS, 128)) * roll(state, 64)
    )
    gather = (iota((128, 128), 0) // 16 == iota((128, 128), 1) // 16).astype(BF16)
    spread = sum(dot_nt(gather, jnp.concatenate([part] * 16, 0)) for part in thirds(state))
    couple_grid = jnp.concatenate([third[64 * k : 64 * k + 64] for k in range(4)], 1)
    k_re, k_im = couple_grid * spread[:64], couple_grid * spread[64:]
    left = jnp.concatenate(
        [jnp.concatenate([k_re, -k_im], 1), jnp.concatenate([k_im, k_re], 1)], 0
    )
    left_high, left_low = halves(left)
    wrapped = dot(jnp.concatenate([left_high, left_low], 0), resonances[:1024])
    wrapped = (wrapped[:128] + wrapped[128:]) + dot(left_high, resonances[1024:])
    turned = spectrum.T
    re, im = turned[:64], turned[64:]
    gain = jnp.concatenate([third[256:384], third[384:512]], 1)
    gain_re, gain_im = gain[:64], gain[64:]
    out_re = re + (re * gain_re - im * gain_im) + wrapped[:64]
    out_im = im + (re * gain_im + im * gain_re) + wrapped[64:]
    both = jnp.concatenate(
        [jnp.concatenate([out_re, -out_im], 1), jnp.concatenate([out_im, out_re], 1)], 0
    )
    high, low = halves(both)
    mixed = dot(jnp.concatenate([high, low], 0), back[:512])
    mixed = (mixed[:128] + mixed[128:]) + dot(high, back[512:1024])
    re, im = mixed[:64], mixed[64:]
    tc, ts = untwist(shift[512:])
    re, im = re * tc - im * ts, im * tc + re * ts
    mixed = jnp.concatenate(
        [re[:, :128], im[:, :128], re[:, 128:], im[:, 128:]], 0
    ) * (1.0 / NT)
    return table_times(back[1024:], mixed)


def lane_roll(value, shift):
    return pltpu.roll(value, shift, 1)


def shape(*dims, dtype=F32):
    return jax.ShapeDtypeStruct(dims, dtype)


VMEM_SPEC = pl.BlockSpec(memory_space=pltpu.VMEM)
HBM_SPEC = pl.BlockSpec(memory_space=pltpu.HBM)


def call(kernel, out_shape, in_specs, out_specs, scratch, *operands, flops, limit=40):
    moved = sum(x.size * x.dtype.itemsize for x in operands)
    return pl.pallas_call(
        kernel,
        out_shape=out_shape,
        in_specs=in_specs,
        out_specs=out_specs,
        scratch_shapes=scratch,
        compiler_params=pltpu.CompilerParams(vmem_limit_bytes=limit * 1024 * 1024),
        cost_estimate=pl.CostEstimate(flops=flops, bytes_accessed=moved, transcendentals=0),
    )(*operands)


def halves_of_tiles(upper, lower):
    low = iota((8, 128), 0) < 4
    return (
        jnp.where(low, upper, pltpu.roll(lower, 4, 0)),
        jnp.where(low, pltpu.roll(upper, 4, 0), lower),
    )


def cut_kernel(field, out):
    for c in range(2):
        for row in range(8):
            tile = field[c, 8 * row : 8 * row + 8, :]
            first, second = halves_of_tiles(tile[:, :128], tile[:, 128:])
            out[32 * row + 8 * c : 32 * row + 8 * c + 8, :] = first
            out[32 * row + 16 + 8 * c : 32 * row + 24 + 8 * c, :] = second


def join_kernel(rows, field, buffer, sems):
    copies = []
    for c in range(2):
        for row in range(8):
            first = rows[32 * row + 8 * c : 32 * row + 8 * c + 8, :]
            second = rows[32 * row + 16 + 8 * c : 32 * row + 24 + 8 * c, :]
            upper, lower = halves_of_tiles(first, second)
            buffer[c, 8 * row : 8 * row + 8, :128] = upper
            buffer[c, 8 * row : 8 * row + 8, 128:] = lower
        copies.append(pltpu.make_async_copy(buffer.at[c], field.at[c], sems.at[c]))
        copies[-1].start()
    for copy in copies:
        copy.wait()


PREPARED = (shape(2560, 256, dtype=BF16), shape(2136, 128))


def prepare_kernel(packed, tables, later):
    quad = lax.axis_index("tm")
    here = lax.axis_index("lat") * 16 + quad
    packed = packed[...]
    made = prepare_first(packed, quad)
    second, second_tables, third = prepare_rest(packed, made, here, quad)
    tables[:2048] = made[0]
    tables[2048:] = second_tables
    later[:1040] = second
    later[1040:1616] = third
    later[1616:] = made[1]


def rows_kernel(field, tables, later, ahead, out):
    spectrum, *rest = to_rows(
        field[...], later[1616:], tables.at[:2048], ahead, lane_roll
    )
    out[pl.ds(0, 256, stride=4), :] = spectrum
    for k, row in enumerate(rest):
        out[pl.ds(k + 1, 256, stride=4), :] = jnp.broadcast_to(row, (256, 128))


def columns_kernel(message, ahead, tables, later, out):
    parts = [message[pl.ds(k, 256, stride=4), :] for k in range(4)]
    out[...] = columns_step(parts, ahead[:, :512], later, tables[2048:], lane_roll)


def blocks_kernel(spectrum, tables, later, back, shift, out):
    out[...] = to_blocks(
        spectrum[...], tables[:2048], later[1040:1616], back[...], shift[...], lane_roll
    )


def on_device(
    light_field, lateral_phase, spectral_phase, occupation, bin_decay, bin_detune, group_bin
):
    t = {name: jnp.asarray(value) for name, value in TABLES.items()}
    sems = pltpu.SemaphoreType.DMA
    rows = call(
        cut_kernel, shape(256, 128), [VMEM_SPEC], VMEM_SPEC, [], light_field, flops=1000
    )
    rows = lax.all_to_all(rows.reshape(16, 16, 128), "tm", 0, 0, tiled=True)
    packed = pack(
        bin_decay, bin_detune, group_bin, spectral_phase, lateral_phase, occupation
    )
    tables, later = call(
        prepare_kernel, PREPARED, [VMEM_SPEC], (VMEM_SPEC,) * 2, [], packed, flops=4_000_000_000
    )
    message = call(
        rows_kernel, shape(1024, 128), [VMEM_SPEC] * 4, VMEM_SPEC, [],
        rows.reshape(256, 128), tables, later, t["ahead"],
        flops=1_500_000_000,
    )
    message = lax.all_to_all(message.reshape(256, 4, 128), BOTH, 0, 0, tiled=True)
    columns = call(
        columns_kernel, shape(256, 128), [VMEM_SPEC] * 4, VMEM_SPEC, [],
        message.reshape(1024, 128), t["ahead"], tables, later, flops=3_000_000_000,
    )
    spectrum = lax.all_to_all(columns, BOTH, 0, 0, tiled=True)
    finished = call(
        blocks_kernel, shape(256, 128), [VMEM_SPEC] * 5, VMEM_SPEC, [],
        spectrum, tables, later, t["back"], t["shift"], flops=2_300_000_000,
    )
    turned = lax.all_to_all(finished.reshape(16, 16, 128), "tm", 0, 0, tiled=True)
    return call(
        join_kernel, shape(2, 64, 256), [VMEM_SPEC], HBM_SPEC,
        [pltpu.VMEM((2, 64, 256), F32), sems((2,))], turned.reshape(256, 128), flops=1000,
    )


def solution(mesh):
    return jax.shard_map(
        on_device,
        mesh=mesh,
        in_specs=(P(None, "lat", "tm"), P(), P(), P(None, "lat"), P(), P(), P()),
        out_specs=P(None, "lat", "tm"),
        check_vma=False,
    )
```

```python
import math

import jax
import jax.numpy as jnp
import numpy as np
from jax import lax
from jax.experimental import pallas as pl
from jax.experimental.pallas import tpu as pltpu
from jax.sharding import PartitionSpec as P

NX, NT, BINS, GROUPS = 1024, 4096, 32, 128
WEIGHT = 0.5 / math.sqrt(GROUPS)
F32, BF16 = jnp.float32, jnp.bfloat16
BOTH = ("lat", "tm")


def split_table(table):
    high = table.astype(np.float32).astype(jnp.bfloat16)
    low = (table - high.astype(np.float64)).astype(jnp.bfloat16)
    return high, low


def build_tables():
    grid = np.arange
    angle = 2 * np.pi * (grid(256)[:, None] * grid(256)[None, :] % 256) / 256
    wide = np.concatenate([np.cos(angle), np.sin(angle)], 1)
    tall = np.concatenate([np.cos(angle), np.sin(angle)], 0)
    lane = grid(128)
    c, q, col = lane // 64, lane // 16 % 4, lane % 16
    to, row = grid(256), grid(256)
    th, tc, tq, tw = to // 128, to // 64 % 2, to // 16 % 4, to % 16
    rm, rc, rh, rq = row // 16, row // 8 % 2, row // 4 % 2, row % 4
    turn = 2 * np.pi * (tw[:, None] * rm[None, :] % 16) / 16
    sign = np.where(tc[:, None] == 0, 1.0, -1.0)
    small = np.where(tc[:, None] == rc[None, :], np.cos(turn), sign * np.sin(turn))
    small = small * (tq[:, None] == rq[None, :]) * (th[:, None] == rh[None, :])
    short = 2 * np.pi * (col[:64, None] * grid(256)[None, :]) / NT
    omega_lanes = np.tile(2 * np.pi * (16 * grid(256)[:, None] + grid(16)[None, :]) / NT, (1, 8))
    t = {}
    t["ahead"] = np.concatenate(
        [np.concatenate(split_table(x), 0) for x in (wide, small)], 1
    )
    t["back"] = np.concatenate(split_table(tall) + split_table(small.T), 0)
    twist = np.concatenate([np.cos(short), np.sin(short)], 0)
    omega_part = np.concatenate([np.cos(omega_lanes), -np.sin(omega_lanes)], 0)
    twist = [twist[:, :128], twist[:, 128:]]
    t["shift"] = np.concatenate([omega_part / NT] + twist, 0).astype(np.float32)
    return t


STEP = 2 * math.pi / NT
STEP_HIGH = round(STEP * 2**22) / 2**22
STEP_LOW = STEP - STEP_HIGH
TURN = (6.28125, 2 * math.pi - 6.28125)
TABLES = build_tables()


def iota(shape, dim):
    return lax.broadcasted_iota(jnp.int32, shape, dim)


def halves(value):
    high = value.astype(BF16)
    return high, (value - high.astype(F32)).astype(BF16)


def thirds(value):
    high = value.astype(BF16)
    rest = value - high.astype(F32)
    middle = rest.astype(BF16)
    return high, middle, (rest - middle.astype(F32)).astype(BF16)


def dot(left, right):
    return lax.dot_general(left, right, (((1,), (0,)), ((), ())), preferred_element_type=F32)


def dot_nt(left, right):
    return lax.dot_general(left, right, (((1,), (1,)), ((), ())), preferred_element_type=F32)


def quadrants(product, rows, cols):
    rest = product[:rows, cols:] + (product[rows:, :cols] + product[rows:, cols:])
    return product[:rows, :cols] + rest


def table_times(table, value):
    product = dot(table, jnp.concatenate(halves(value), 1))
    return quadrants(product, table.shape[0] // 2, value.shape[1])


def times_table(value, table):
    product = dot(jnp.concatenate(halves(value), 0), table)
    return quadrants(product, value.shape[0], table.shape[1] // 2)


def sine_cosine_half(angle):
    x = angle * 0.5
    z = x * x
    s = jnp.full_like(z, 1.0 / 6227020800.0)
    for k in (-1.0 / 39916800.0, 1.0 / 362880.0, -1.0 / 5040.0, 1.0 / 120.0, -1.0 / 6.0):
        s = s * z + k
    c = jnp.full_like(z, -1.0 / 87178291200.0)
    for k in (1.0 / 479001600.0, -1.0 / 3628800.0, 1.0 / 40320.0, -1.0 / 720.0, 1.0 / 24.0, -0.5):
        c = c * z + k
    return x + x * (z * s), 1.0 + z * c


def resonance(detune, keep, lost, index):
    index = jnp.where(index > NT // 2, index - NT, index).astype(F32)
    s, c = sine_cosine_half((detune + index * STEP_HIGH) + index * STEP_LOW)
    re = lost + (2.0 * keep) * (s * s)
    im = (2.0 * keep) * (s * c)
    scale = 1.0 / (re * re + im * im)
    return re * scale, -(im * scale)


def cosine_sine(angle):
    s, c = sine_cosine_half(angle)
    return 1.0 - 2.0 * (s * s), 2.0 * (s * c)


def lost_by(rate):
    total = jnp.full_like(rate, 1.0 / 5040.0)
    for k in (-1.0 / 720.0, 1.0 / 120.0, -1.0 / 24.0, 1.0 / 6.0, -0.5, 1.0):
        total = k + rate * total
    return rate * total


def exact_dot(left, right):
    parts = thirds(left)
    return (dot(parts[0], right) + dot(parts[1], right)) + dot(parts[2], right)


def pick_dot(left, right):
    parts = thirds(right)
    return (dot(left, parts[0]) + dot(left, parts[1])) + dot(left, parts[2])


def pick_dot_nt(left, right):
    parts = thirds(right)
    return (dot_nt(left, parts[0]) + dot_nt(left, parts[1])) + dot_nt(left, parts[2])


def bin_columns(decay, detune):
    lost = lost_by(decay)
    keep = 1.0 - lost
    drive = jnp.sqrt(lost_by(2.0 * decay))
    cos, sin = cosine_sine(detune)
    p_re, p_im = keep * cos, -keep * sin
    whole = jnp.exp(-float(NT) * decay)
    far = float(NT) * detune
    turns = jnp.floor(far * (0.5 / math.pi) + 0.5)
    cos, sin = cosine_sine((far - turns * TURN[0]) - turns * TURN[1])
    r_re, r_im = 1.0 - whole * cos, whole * sin
    k_re, k_im = p_re * r_re - p_im * r_im, p_re * r_im + p_im * r_re
    rows = jnp.concatenate(
        [detune, keep, lost, drive, WEIGHT * k_im, -WEIGHT * k_re, keep, keep], 0
    )
    eye = (iota((BINS, BINS), 0) == iota((BINS, BINS), 1)).astype(BF16)
    return pick_dot_nt(eye, rows)


def pack(decay, detune, group_bin, spectral, lateral, occupation):
    parts = [decay, detune, group_bin, spectral, lateral, occupation.T.reshape(-1)]
    starts = [0, BINS, 128, 256, 256 + NT, 256 + NT + NX]
    total = starts[-1] + parts[-1].size
    padded = [
        jnp.pad(part, (start, total - start - part.size)).astype(F32) for part, start in zip(parts, starts)
    ]
    return sum(padded[1:], padded[0]).reshape(total // 128, 128)


def unpack(packed):
    return (packed[0:1, :BINS], packed[0:1, BINS : 2 * BINS], packed[1:2], packed[2:34],
            packed[34:42], packed[42:])


def couplings(drive, group_bin, occupation):
    member = (iota((BINS, GROUPS), 0).astype(F32) == group_bin).astype(BF16)
    return pick_dot_nt(member, occupation) * drive


def prepare_first(packed, quad):
    decay, detune_row, group_bin, spectral, _, occupation = unpack(packed)
    params = bin_columns(decay, detune_row)
    detune, keep, lost, drive = (params[:, k : k + 1] for k in range(4))
    real, imag = [], []
    for w1 in range(16):
        g_re, g_im = resonance(detune, keep, lost, 16 * iota((BINS, 256), 1) + w1)
        real.append(g_re)
        imag.append(g_im)
    resonances = jnp.concatenate(halves(jnp.concatenate(real + imag, 0)), 0)
    per_bin = couplings(drive, group_bin, occupation)
    points = occupation.shape[0]
    pick = iota((points, 128), 0) == 4 * quad + iota((points, 128), 1) // 16 % 4
    chosen = exact_dot(per_bin, pick.astype(BF16))
    lane = iota((BINS, 128), 1)
    couple_row = jnp.sum(
        jnp.where(iota((BINS, 128), 0) == lane // 64 * 16 + lane % 16, chosen, 0.0),
        axis=0, keepdims=True,
    )
    cos, sin = cosine_sine(spectral)
    spectral_parts = cos, sin
    row_of = (iota((256, 32), 0) // 8 == iota((256, 32), 1)).astype(BF16)
    mine = iota((256, 128), 1) // 16 == iota((256, 128), 0) % 8
    lane_of = (iota((128, 128), 0) % 16 == iota((128, 128), 1) % 16).astype(BF16)
    cos = exact_dot(jnp.where(mine, pick_dot(row_of, cos), 0.0), lane_of)
    sin = exact_dot(jnp.where(mine, pick_dot(row_of, sin), 0.0), lane_of)
    index = 16 * iota((256, 128), 0) + iota((256, 128), 1) % 16
    back_re, back_im = cosine_sine(jnp.where(index > NT // 2, NT - index, -index) * STEP)
    wrap_a = (cos * back_re - sin * back_im) * (1.0 / NT)
    wrap_b = (cos * back_im + sin * back_re) * (1.0 / NT)
    index = (iota((64, 256), 0) % 16) * iota((64, 256), 1)
    tc, ts = cosine_sine(jnp.where(index > NT // 2, index - NT, index).astype(F32) * STEP)
    first = jnp.concatenate(
        [tc[:, :128], ts[:, :128], tc[:, 128:], ts[:, 128:],
         jnp.where(iota((256, 128), 1) < 64, wrap_a, wrap_b),
         jnp.broadcast_to(couple_row, (8, 128))],
        0,
    )
    return resonances, first, params, per_bin, spectral_parts


def prepare_rest(packed, made, here, quad):
    lateral = unpack(packed)[4]
    resonances, _, params, per_bin, (cos, sin) = made
    points = per_bin.shape[1]
    pick_rows = iota((64, points), 1) == 4 * quad + iota((64, points), 0) // 16
    spread = pick_dot_nt(pick_rows.astype(BF16), jnp.concatenate([per_bin] * 16, 0))
    couple_grid = jnp.where(
        iota((64, 512), 1) // 32 == iota((64, 512), 0) % 16, spread, 0.0
    )
    gain_high, gain_low = halves(couple_grid * WEIGHT)
    gain = dot(jnp.concatenate([gain_high, gain_low], 0),
               jnp.concatenate([resonances[:512], resonances[512:1024]], 1))
    gain_rest = dot(gain_high, jnp.concatenate([resonances[1024:1536], resonances[1536:]], 1))
    gain = (gain[:64] + gain[64:]) + gain_rest
    gain = jnp.concatenate([-gain[:, 256:], gain[:, :256]], 0)
    own = (iota((32, 128), 0) == here // 8) & (iota((32, 128), 1) // 16 == here % 8)
    lane_of = (iota((128, 128), 0) % 16 == iota((128, 128), 1) % 16).astype(BF16)
    own_rows = [jnp.sum(jnp.where(own, x, 0.0), axis=0, keepdims=True) for x in (cos, sin)]
    own_rows = exact_dot(jnp.concatenate(own_rows * 4, 0), lane_of)
    once_re, once_im = own_rows[0:1], own_rows[1:2]
    eye = (iota((128, 128), 0) == iota((128, 128), 1)).astype(BF16)
    cos, sin = cosine_sine(lateral)
    cos, sin = pick_dot_nt(eye, cos), pick_dot_nt(eye, sin)
    r, i = (
        [
            jnp.concatenate([x[:, 2 * k : 2 * k + 1], x[:, 2 * k + 1 : 2 * k + 2]], 0)
            for k in range(4)
        ]
        for x in (cos, sin)
    )
    blocks_re = [
        (r[0] + r[2]) + (r[1] + r[3]),
        (r[0] - r[2]) + (i[1] - i[3]),
        (r[0] + r[2]) - (r[1] + r[3]),
        (r[0] - r[2]) - (i[1] - i[3]),
    ]
    blocks_im = [
        (i[0] + i[2]) + (i[1] + i[3]),
        (i[0] - i[2]) - (r[1] - r[3]),
        (i[0] + i[2]) - (i[1] + i[3]),
        (i[0] - i[2]) + (r[1] - r[3]),
    ]
    eight = iota((256, 128), 1) // 16
    index = iota((256, 128), 0)
    cos1, sin1 = cosine_sine(index.astype(F32) * (-2.0 * math.pi / NX))
    cos2, sin2 = cos1 * cos1 - sin1 * sin1, 2.0 * (cos1 * sin1)
    cos3, sin3 = cos1 * cos2 - sin1 * sin2, cos1 * sin2 + sin1 * cos2
    turns = [None, (cos1, sin1), (cos2, sin2), (cos3, sin3)]
    mixing = []
    for k in range(4):
        re, im = blocks_re[k] * (1.0 / NX), blocks_im[k] * (1.0 / NX)
        if k == 0:
            real, imag = re, im
        else:
            near = eight % 4 + k < 4
            cos = jnp.where(near, turns[k][0], turns[4 - k][0])
            sin = jnp.where(near, turns[k][1], -turns[4 - k][1])
            real, imag = cos * re - sin * im, cos * im + sin * re
        mixing.append(jnp.where(eight < 4, real, imag))
    mixing = jnp.concatenate(mixing, 0)
    rows = jnp.concatenate([params[:16]] * 4 + [params[16:]] * 4, 0)
    g_re, g_im = resonance(
        rows[:, 0:1], rows[:, 1:2], rows[:, 2:3], 16 * here + iota((128, 128), 1) % 16
    )
    twice_re = once_re * once_re - once_im * once_im
    twice_im = 2.0 * once_re * once_im
    inside = iota((128, 128), 0) // 16 % 4 == iota((128, 128), 1) // 16 % 4
    left = iota((128, 128), 1) < 64
    f_re, f_im = -WEIGHT * twice_im, WEIGHT * twice_re
    b_re = jnp.where(inside, g_re * f_re - g_im * f_im, 0.0)
    b_im = jnp.where(inside, g_re * f_im + g_im * f_re, 0.0)
    gain_here = jnp.concatenate([b_re, jnp.where(left, -b_im, b_im)], 1)
    gain_here = jnp.concatenate(halves(gain_here), 0)
    side_row = jnp.where(iota((1, 128), 1) < 64, -1.0, 1.0)
    twice = jnp.concatenate([twice_re] * 8 + [twice_im * side_row] * 8, 0)
    k_re, k_im = rows[:, 4:5], rows[:, 5:6]
    f_re = once_re * k_re - once_im * k_im
    f_im = once_re * k_im + once_im * k_re
    h_re = jnp.where(inside, g_re * f_re - g_im * f_im, 0.0)
    h_im = jnp.where(inside, g_re * f_im + g_im * f_re, 0.0)
    top, bottom = jnp.where(left, h_re, h_im), jnp.where(left, -h_im, h_re)
    wrap_here = jnp.concatenate([top[:64], bottom[:64], top[64:], bottom[64:]], 0)
    wrap_here = jnp.concatenate(halves(wrap_here), 1)
    second = jnp.concatenate([twice, mixing], 0)
    second_tables = jnp.concatenate([gain_here, wrap_here], 0)
    turned = [jnp.broadcast_to(params[:, k : k + 1], (BINS, 128)) for k in (4, 5)]
    third = jnp.concatenate(
        [couple_grid[:, 128 * k : 128 * k + 128] for k in range(4)]
        + [gain[:, :128], gain[:, 128:]] + turned, 0,
    )
    return second, second_tables, third


def half_sign(shape):
    return jnp.where(iota(shape, 1) < 64, -1.0, 1.0)


def wrap_state(resonances, weighted, roll):
    product = dot(resonances, jnp.concatenate(halves(weighted), 1))
    product = quadrants(product, 1024, 128)
    lane = iota((BINS, 128), 1) % 16
    sums = []
    for part in range(2):
        total = jnp.zeros((BINS, 128), F32)
        for w1 in range(16):
            start = (part * 16 + w1) * BINS
            total = jnp.where(lane == w1, product[start : start + BINS], total)
        sums.append(total)
    return sums[0] + half_sign((BINS, 128)) * roll(sums[1], 64)


def unfold(pair, roll):
    turned = roll(pair, 64)
    left = iota((256, 128), 1) < 64
    return jnp.where(left, pair, turned), jnp.where(left, -turned, pair)


def untwist(pair):
    return (jnp.concatenate([pair[k : k + 64], pair[128 + k : 192 + k]], 1) for k in (0, 64))


def to_rows(field, first, resonances, ahead, roll):
    mixed = table_times(ahead[:, 512:], field)
    mixed = jnp.concatenate([mixed[:128], mixed[128:]], 1)
    re, im = mixed[:64], mixed[64:]
    tc, ts = untwist(first)
    re, im = re * tc + im * ts, im * tc - re * ts
    both = jnp.concatenate(
        [jnp.concatenate([re, im], 1), jnp.concatenate([im, -re], 1)], 0
    )
    product = dot_nt(ahead[:, :512], jnp.concatenate(halves(both), 0))
    spectrum = quadrants(product, 256, 128)
    wrap_a, wrap_b = unfold(first[256:512], roll)
    weighted = wrap_a * spectrum + wrap_b * roll(spectrum, 64)
    state = wrap_state(resonances[...], weighted, roll)
    place = (iota((128, 256), 0) // 16 == iota((128, 256), 1) % 128 // 16).astype(BF16)
    parts = exact_dot(state, place)
    lane = iota((BINS, 256), 1)
    chosen = iota((BINS, 256), 0) == lane // 128 * 16 + lane % 16
    state_row = jnp.sum(jnp.where(chosen, parts, 0.0), axis=0, keepdims=True)
    return spectrum, state_row[:, :128], state_row[:, 128:], first[512:513]


def diffract(blocks, wide, mixing, roll):
    sign = half_sign((256, 128))

    def transform(parts, direction):
        columns = []
        for part in parts:
            turned = roll(part, 64) * (sign * (-direction))
            columns += list(halves(jnp.concatenate([part, turned], 0)))
        product = dot(wide, jnp.concatenate(columns, 1))
        return [
            quadrants(product[:, 256 * k : 256 * k + 256], 256, 128) for k in range(len(parts))
        ]

    spectra = transform(blocks, 1.0)
    mixed = []
    for part in spectra:
        total = mixing[0] * part
        for r in range(1, 8):
            total = total + mixing[r] * roll(part, 128 - 16 * r)
        mixed.append(total)
    return transform(mixed, -1.0)


def columns_step(message, wide, second, second_tables, roll):
    field, state0, state1, couple = message
    eight = iota((256, 128), 1) // 16
    mixing = [None] * 8
    for k in range(4):
        real, imag = unfold(second[16 + 256 * k : 272 + 256 * k], roll)
        for r in (k, k + 4):
            mixing[r] = jnp.where((eight + r) % 8 // 4 == eight // 4, real, imag)
    field, state0, state1 = diffract([field, state0, state1], wide, mixing, roll)
    product = dot(jnp.concatenate(halves(couple), 0), second_tables[:128])
    rest = dot(couple.astype(BF16), second_tables[128:256])
    factor = (product[:256] + product[256:]) + rest
    turned = roll(couple, 64)
    left = iota((256, 128), 1) < 64
    states = jnp.concatenate(
        [state0 * jnp.where(left, couple, turned), state1 * jnp.where(left, turned, couple)], 1
    )
    wrapped = times_table(states, second_tables[256:])
    straight, crossed = factor[:, :128] + second[0:1], factor[:, 128:] + second[8:9]
    field = straight * field + crossed * roll(field, 64) + wrapped
    return diffract([field], wide, mixing, roll)[0]


def to_blocks(spectrum, resonances, third, back, shift, roll):
    sign = half_sign((256, 128))
    weighted = shift[:256] * spectrum + (shift[256:512] * sign) * roll(spectrum, 64)
    state = wrap_state(resonances[...], weighted, roll)
    state = third[512:544] * state + third[544:576] * (
        half_sign((BINS, 128)) * roll(state, 64)
    )
    gather = (iota((128, 128), 0) // 16 == iota((128, 128), 1) // 16).astype(BF16)
    spread = sum(dot_nt(gather, jnp.concatenate([part] * 4, 0)) for part in thirds(state))
    spread = jnp.concatenate([spread] * 4, 1)
    couple_grid = jnp.concatenate([third[64 * k : 64 * k + 64] for k in range(4)], 1)
    k_re, k_im = couple_grid * spread[:64], couple_grid * spread[64:]
    left = jnp.concatenate(
        [jnp.concatenate([k_re, -k_im], 1), jnp.concatenate([k_im, k_re], 1)], 0
    )
    left_high, left_low = halves(left)
    wrapped = dot(jnp.concatenate([left_high, left_low], 0), resonances[:1024])
    wrapped = (wrapped[:128] + wrapped[128:]) + dot(left_high, resonances[1024:])
    turned = spectrum.T
    re, im = turned[:64], turned[64:]
    gain = jnp.concatenate([third[256:384], third[384:512]], 1)
    gain_re, gain_im = gain[:64], gain[64:]
    out_re = re + (re * gain_re - im * gain_im) + wrapped[:64]
    out_im = im + (re * gain_im + im * gain_re) + wrapped[64:]
    both = jnp.concatenate(
        [jnp.concatenate([out_re, -out_im], 1), jnp.concatenate([out_im, out_re], 1)], 0
    )
    high, low = halves(both)
    mixed = dot(jnp.concatenate([high, low], 0), back[:512])
    mixed = (mixed[:128] + mixed[128:]) + dot(high, back[512:1024])
    re, im = mixed[:64], mixed[64:]
    tc, ts = untwist(shift[512:])
    re, im = re * tc - im * ts, im * tc + re * ts
    mixed = jnp.concatenate(
        [re[:, :128], im[:, :128], re[:, 128:], im[:, 128:]], 0
    ) * (1.0 / NT)
    return table_times(back[1024:], mixed)


def lane_roll(value, shift):
    return pltpu.roll(value, shift, 1)


def shape(*dims, dtype=F32):
    return jax.ShapeDtypeStruct(dims, dtype)


VMEM_SPEC = pl.BlockSpec(memory_space=pltpu.VMEM)
HBM_SPEC = pl.BlockSpec(memory_space=pltpu.HBM)


def call(kernel, out_shape, in_specs, out_specs, scratch, *operands, flops, limit=40):
    moved = sum(x.size * x.dtype.itemsize for x in operands)
    return pl.pallas_call(
        kernel,
        out_shape=out_shape,
        in_specs=in_specs,
        out_specs=out_specs,
        scratch_shapes=scratch,
        compiler_params=pltpu.CompilerParams(vmem_limit_bytes=limit * 1024 * 1024),
        cost_estimate=pl.CostEstimate(flops=flops, bytes_accessed=moved, transcendentals=0),
    )(*operands)


def halves_of_tiles(upper, lower):
    low = iota((8, 128), 0) < 4
    return (
        jnp.where(low, upper, pltpu.roll(lower, 4, 0)),
        jnp.where(low, pltpu.roll(upper, 4, 0), lower),
    )


def cut_kernel(field, out):
    for c in range(2):
        for row in range(8):
            tile = field[c, 8 * row : 8 * row + 8, :]
            first, second = halves_of_tiles(tile[:, :128], tile[:, 128:])
            out[32 * row + 8 * c : 32 * row + 8 * c + 8, :] = first
            out[32 * row + 16 + 8 * c : 32 * row + 24 + 8 * c, :] = second


def join_kernel(rows, field, buffer, sems):
    copies = []
    for c in range(2):
        for row in range(8):
            first = rows[32 * row + 8 * c : 32 * row + 8 * c + 8, :]
            second = rows[32 * row + 16 + 8 * c : 32 * row + 24 + 8 * c, :]
            upper, lower = halves_of_tiles(first, second)
            buffer[c, 8 * row : 8 * row + 8, :128] = upper
            buffer[c, 8 * row : 8 * row + 8, 128:] = lower
        copies.append(pltpu.make_async_copy(buffer.at[c], field.at[c], sems.at[c]))
        copies[-1].start()
    for copy in copies:
        copy.wait()


PREPARED = (shape(2560, 256, dtype=BF16), shape(2136, 128))


def prepare_kernel(packed, tables, later):
    quad = lax.axis_index("tm")
    here = lax.axis_index("lat") * 16 + quad
    packed = packed[...]
    made = prepare_first(packed, quad)
    second, second_tables, third = prepare_rest(packed, made, here, quad)
    tables[:2048] = made[0]
    tables[2048:] = second_tables
    later[:1040] = second
    later[1040:1616] = third
    later[1616:] = made[1]


def rows_kernel(field, tables, later, ahead, out):
    spectrum, *rest = to_rows(
        field[...], later[1616:], tables.at[:2048], ahead, lane_roll
    )
    out[pl.ds(0, 256, stride=4), :] = spectrum
    for k, row in enumerate(rest):
        out[pl.ds(k + 1, 256, stride=4), :] = jnp.broadcast_to(row, (256, 128))


def columns_kernel(message, ahead, tables, later, out):
    parts = [message[pl.ds(k, 256, stride=4), :] for k in range(4)]
    out[...] = columns_step(parts, ahead[:, :512], later, tables[2048:], lane_roll)


def blocks_kernel(spectrum, tables, later, back, shift, out):
    out[...] = to_blocks(
        spectrum[...], tables[:2048], later[1040:1616], back[...], shift[...], lane_roll
    )


def on_device(
    light_field, lateral_phase, spectral_phase, occupation, bin_decay, bin_detune, group_bin
):
    t = {name: jnp.asarray(value) for name, value in TABLES.items()}
    sems = pltpu.SemaphoreType.DMA
    rows = call(
        cut_kernel, shape(256, 128), [VMEM_SPEC], VMEM_SPEC, [], light_field, flops=1000
    )
    rows = lax.all_to_all(rows.reshape(16, 16, 128), "tm", 0, 0, tiled=True)
    packed = pack(
        bin_decay, bin_detune, group_bin, spectral_phase, lateral_phase, occupation
    )
    tables, later = call(
        prepare_kernel, PREPARED, [VMEM_SPEC], (VMEM_SPEC,) * 2, [], packed, flops=4_000_000_000
    )
    message = call(
        rows_kernel, shape(1024, 128), [VMEM_SPEC] * 4, VMEM_SPEC, [],
        rows.reshape(256, 128), tables, later, t["ahead"],
        flops=1_500_000_000,
    )
    message = lax.all_to_all(message.reshape(256, 4, 128), BOTH, 0, 0, tiled=True)
    columns = call(
        columns_kernel, shape(256, 128), [VMEM_SPEC] * 4, VMEM_SPEC, [],
        message.reshape(1024, 128), t["ahead"], tables, later, flops=3_000_000_000,
    )
    spectrum = lax.all_to_all(columns, BOTH, 0, 0, tiled=True)
    finished = call(
        blocks_kernel, shape(256, 128), [VMEM_SPEC] * 5, VMEM_SPEC, [],
        spectrum, tables, later, t["back"], t["shift"], flops=2_300_000_000,
    )
    turned = lax.all_to_all(finished.reshape(16, 16, 128), "tm", 0, 0, tiled=True)
    return call(
        join_kernel, shape(2, 64, 256), [VMEM_SPEC], HBM_SPEC,
        [pltpu.VMEM((2, 64, 256), F32), sems((2,))], turned.reshape(256, 128), flops=1000,
    )


def solution(mesh):
    return jax.shard_map(
        on_device,
        mesh=mesh,
        in_specs=(P(None, "lat", "tm"), P(), P(), P(None, "lat"), P(), P(), P()),
        out_specs=P(None, "lat", "tm"),
        check_vma=False,
    )
```
